1024 devices in a mesh: gx: 8 (over y_hi, x), gy: 8 (over y_lo, core), gz: 16 (over z).
Axes of the slice: x: 4, y: 8 (y_hi: 2, y_lo: 4; y = y_hi * 4 + y_lo), z: 16, core: 2. Of those that a mesh axis runs over, the one named last changes fastest.
Arguments:
- e_field: float32 [3, 64, 64, 2048], P(None, 'gx', 'gy', 'gz'), may hold values from -6 to 6
- material: int32 [64, 64, 2048], P('gx', 'gy', 'gz'), may hold values from 0 to 15
- permittivity: float32 [16], replicated, may hold values from 1 to 8
- loss: float32 [16], replicated, may hold values from 0 to 0.5
- port_cell: int32 [16384], P(('gx', 'gy', 'gz')), may hold values from 0 to 8191, as said below
- port_owner: int32 [16384, 1], P(('gx', 'gy', 'gz')), may hold values from 0 to 15; in each aligned block of 16 rows (0 to 15, 16 to 31, ...) at most 2 rows name the same one
- circuit_block: int32 [32768], P(('gx', 'gy', 'gz')), may hold values from 0 to 1
- circuit_state: float32 [32768, 256], P(('gx', 'gy', 'gz')), may hold values from -6 to 6
- mna_update: float32 [2048, 256, 256], P(('gx', 'gy', 'gz')), as said below
- mna_drive: float32 [2048, 256], P(('gx', 'gy', 'gz')), may hold values from -6 to 6
- mna_sense: float32 [2048, 256], P(('gx', 'gy', 'gz')), may hold values from -0.375 to 0.375
Outputs:
- e_final: float32 [3, 64, 64, 2048], P(None, 'gx', 'gy', 'gz')
- h_final: float32 [3, 64, 64, 2048], P(None, 'gx', 'gy', 'gz')
- circuit_final: float32 [32768, 256], P(('gx', 'gy', 'gz'))
The draws below stay inside these ranges and needn't reach their ends.
Inputs may be any that keep to these rules, and one draw needn't show every extreme that they name: `port_cell`: the 16 ports of one device lie in distinct cells. `port_owner`: among the 16 ports of one device no owner is named more than 2 times. `mna_update`: diagonal entries of each block lie between 0.4 and 0.8; off-diagonal entries are of about 0.3/sqrt(256).
All inputs are finite; a program needn't handle non-finite values.
Results may differ from the reference program's by a relative error of at most 0.0003.
Values sent between devices are 32-bit elements; how exact they have to be, the bound alone decides.
A program may use at most 32 MiB of HBM per device.

```python
import math
import jax
import jax.numpy as jnp
import numpy as np
from jax import lax

CX = 8
CY = 8
CZ = 128
PORT_CAP = 16
NODES = 256
BLK_DEV = 2
NMAT = 16
ITERS = 4
SEND_CAP = 2
NX = 64
NY = 64
NZ = 2048
CELLS_DEV = 8192
PORTS = 16384
OWN_CAP = 32
CIRCUITS = 32768
BLOCKS = 2048
N_GX = 8
N_GY = 8
N_GZ = 16


def draw_port_cell(key, part):
    key = jax.random.fold_in(key, 11)
    keys = jax.random.split(key, PORTS // PORT_CAP)
    picked = jax.vmap(lambda single: jax.random.permutation(single, CELLS_DEV)[:PORT_CAP])(keys)
    return picked.reshape(-1).astype(jnp.int32)


def draw_mna_update(key, part):
    key = jax.random.fold_in(key, 23)
    key_diag, key_off = jax.random.split(key)
    diagonal = jax.random.uniform(key_diag, (BLOCKS, NODES), jnp.float32, 0.4, 0.8)
    offdiag = jax.random.normal(key_off, (BLOCKS, NODES, NODES), jnp.float32)
    identity = jnp.eye(NODES, dtype=jnp.float32)
    return offdiag * (0.3 / NODES ** 0.5) * (1.0 - identity) + diagonal[:, :, None] * identity


def set_ends(entries, rng, least, top_value):
    longest = entries.shape.index(max(entries.shape))
    spots = []
    for shift in (0, 1):
        where = [jax.random.randint(jax.random.fold_in(rng, axis), (), 0, length) for axis, length in enumerate(entries.shape)]
        where[longest] = (where[longest] + shift) % entries.shape[longest]
        spots.append(tuple(where))
    return entries.at[spots[0]].set(least).at[spots[1]].set(top_value)


def level_of(own_key, extent, cuts, smallest, top_value):
    factor_of = 1.0
    for position, parts in cuts:
        draws = jax.random.uniform(jax.random.fold_in(jax.random.fold_in(own_key, 6), position), (parts,), jnp.float32, smallest / len(cuts), top_value / len(cuts))
        factor_of = factor_of * jnp.repeat(jnp.exp(draws), extent[position] // parts).reshape((-1,) + (1,) * (len(extent) - 1 - position))
    return factor_of


def shared_out(rng, own, number, rows, amount, top, limit, slope):
    sequence = jax.random.permutation(rng, amount)
    crowded, usual = shares(amount, rows * top, limit, slope, True), shares(amount, rows * top, limit, slope, False)
    places = jnp.arange(amount)

    def named(sizes, rotation):
        used = int((sizes > 0).sum())
        fixed = max(1, used // 4)
        shifted = fixed + (places - fixed + rotation * (used - fixed)) % max(1, amount - fixed)
        return jnp.zeros((amount,), jnp.int32).at[sequence[jnp.where(places < fixed, places, shifted)]].set(jnp.asarray(sizes, jnp.int32))

    sizes = jnp.where(number % 4 == 0, named(crowded, number // 4), named(usual, number - number // 4 - 1))
    mixed = jax.random.permutation(jax.random.fold_in(own, 3), amount)
    giver, taker = mixed[0:amount // 2 * 2:2], mixed[1:amount // 2 * 2:2]
    margin = jnp.minimum(sizes[giver] - 1, limit - sizes[taker]) // 2
    margin = jnp.where((giver == sequence[0]) | (taker == sequence[0]) | (sizes[taker] == 0), 0, jnp.maximum(margin, 0))
    shifted = jax.random.randint(jax.random.fold_in(own, 4), (amount // 2,), 0, 1 << 20) % (margin + 1)
    sizes = sizes.at[giver].add(-shifted).at[taker].add(shifted)
    labels = jnp.searchsorted(jnp.cumsum(sizes), jnp.arange(rows * top), side="right").astype(jnp.int32)
    table = labels.reshape(top, rows).T
    table = table[jax.random.permutation(jax.random.fold_in(own, 1), rows)]
    rotation = jax.random.randint(jax.random.fold_in(own, 2), (rows, 1), 0, top)
    return jnp.take_along_axis(table, (jnp.arange(top)[None, :] + rotation) % top, axis=1)


def shares(number_of, total, limit, skew, full):
    weights = [(1 << 20) // math.isqrt(rank ** skew) + 1 for rank in range(1, number_of + 1)]
    largest = limit if full else min(limit, max(-(-total // number_of), total * weights[0] // sum(weights)))
    least = 1 if total - largest >= number_of - 1 else 0
    given, spare = [largest] + [least] * (number_of - 1), total - largest - least * (number_of - 1)
    while spare > 0:
        candidates = [i for i in range(1, number_of) if given[i] < largest] or [i for i in range(1, number_of) if given[i] < limit]
        pool, remaining = sum([weights[i] for i in candidates]), spare
        for i in candidates:
            addition = min(limit - given[i], max(1, remaining * weights[i] // pool), spare)
            given[i] = given[i] + addition
            spare = spare - addition
    return np.array(given)


def centred(rng, extent, deviation, reach, shards=(), kind=jnp.bfloat16):
    array = deviation * jax.random.normal(rng, extent, jnp.float32)
    if shards:
        array = array * level_of(rng, extent, shards, -0.22, 0.18)
    return jnp.clip(array, -reach, reach).astype(kind)


def setup_inputs(seed: int = 0) -> dict:
    key_list = jax.random.split(jax.random.key(seed), 12)
    e_field = centred(key_list[0], (3, NX, NY, NZ), 1.0, 6.0, ((1, 8), (2, 8), (3, 16)), jnp.float32)
    material = set_ends(jax.random.randint(key_list[1], (NX, NY, NZ), 0, NMAT), jax.random.fold_in(key_list[1], 1), 0, NMAT - 1).astype(jnp.int32)
    permittivity = jnp.clip(jnp.exp(jax.random.uniform(key_list[2], (NMAT,), jnp.float32, math.log(1.0), math.log(8.0))), 1.0, 8.0)
    loss = jnp.clip(jax.random.uniform(key_list[3], (NMAT,), jnp.float32, 0.0, 0.5), 0.0, 0.5)
    port_cell = draw_port_cell(jax.random.fold_in(key_list[11], 71), 0)
    port_owner_keys = jax.random.split(jax.random.fold_in(key_list[5], 1), PORTS // PORT_CAP)
    port_owner_turns = jax.random.permutation(jax.random.fold_in(key_list[5], 3), PORTS // PORT_CAP)
    port_owner = jax.vmap(lambda own, number: shared_out(jax.random.fold_in(key_list[5], 2), own, number, PORT_CAP, N_GZ, 1, SEND_CAP, 2))(port_owner_keys, port_owner_turns).reshape((PORTS, 1))
    circuit_block = set_ends(jax.random.randint(key_list[6], (CIRCUITS,), 0, BLK_DEV), jax.random.fold_in(key_list[6], 1), 0, BLK_DEV - 1).astype(jnp.int32)
    circuit_state = centred(key_list[7], (CIRCUITS, NODES), 1.0, 6.0, ((0, 1024),), jnp.float32)
    mna_update = draw_mna_update(jax.random.fold_in(key_list[11], 71), 0)
    mna_drive = centred(key_list[9], (BLOCKS, NODES), 1.0, 6.0, ((0, 1024),), jnp.float32)
    mna_sense = centred(key_list[10], (BLOCKS, NODES), NODES ** -0.5, 0.375, ((0, 1024),), jnp.float32)
    return {"e_field": e_field, "material": material, "permittivity": permittivity, "loss": loss, "port_cell": port_cell, "port_owner": port_owner, "circuit_block": circuit_block, "circuit_state": circuit_state, "mna_update": mna_update, "mna_drive": mna_drive, "mna_sense": mna_sense}


def curl_forward(padded):
    base = padded[:, :-1, :-1, :-1]
    plus_x = padded[:, 1:, :-1, :-1]
    plus_y = padded[:, :-1, 1:, :-1]
    plus_z = padded[:, :-1, :-1, 1:]
    comp_x = (plus_y[2] - base[2]) - (plus_z[1] - base[1])
    comp_y = (plus_z[0] - base[0]) - (plus_x[2] - base[2])
    comp_z = (plus_x[1] - base[1]) - (plus_y[0] - base[0])
    return jnp.stack([comp_x, comp_y, comp_z])


def curl_backward(padded):
    base = padded[:, 1:, 1:, 1:]
    minus_x = padded[:, :-1, 1:, 1:]
    minus_y = padded[:, 1:, :-1, 1:]
    minus_z = padded[:, 1:, 1:, :-1]
    comp_x = (base[2] - minus_y[2]) - (base[1] - minus_z[1])
    comp_y = (base[0] - minus_z[0]) - (base[2] - minus_x[2])
    comp_z = (base[1] - minus_x[1]) - (base[0] - minus_y[0])
    return jnp.stack([comp_x, comp_y, comp_z])


def port_slots(owners, groups):
    count = owners.shape[-1]
    onehot = (owners[..., None] == jnp.arange(groups, dtype=jnp.int32)).astype(jnp.float32)
    earlier = (jnp.arange(count)[None, :] < jnp.arange(count)[:, None]).astype(jnp.float32)
    counts = jnp.einsum('pq,dqg->dpg', earlier, onehot)
    return jnp.sum(counts * onehot, axis=-1).astype(jnp.int32)


def circuit_step(state, volts, blocks, update, drive, sense):
    choose = (blocks[None, :] == jnp.arange(update.shape[0], dtype=jnp.int32)[:, None]).astype(jnp.float32)
    product = jnp.einsum('pj,bij->bpi', state, update, precision=lax.Precision.HIGHEST)
    drive_rows = jnp.dot(choose.T, drive, precision=lax.Precision.HIGHEST)
    sense_rows = jnp.dot(choose.T, sense, precision=lax.Precision.HIGHEST)
    fresh = jnp.einsum('bp,bpi->pi', choose, product, precision=lax.Precision.HIGHEST) + drive_rows * volts[:, None]
    current = jnp.sum(fresh * sense_rows, axis=1)
    return fresh, current


def reference(e_field, material, permittivity, loss, port_cell, port_owner, circuit_block, circuit_state, mna_update, mna_drive, mna_sense):
    devices = N_GX * N_GY * N_GZ
    e_keep = ((1.0 - loss) / (1.0 + loss))[material]
    e_gain = (0.5 / (permittivity * (1.0 + loss)))[material]
    cells = port_cell.reshape(devices, PORT_CAP)
    owners = port_owner.reshape(devices, PORT_CAP)
    slot_index = port_slots(owners, N_GZ)
    device_ids = jnp.arange(devices, dtype=jnp.int32)[:, None]
    index_x = device_ids // (N_GY * N_GZ)
    index_y = (device_ids // N_GZ) % N_GY
    index_z = device_ids % N_GZ
    glob_x = (index_x * CX + cells // (CY * CZ)).reshape(-1)
    glob_y = (index_y * CY + (cells // CZ) % CY).reshape(-1)
    glob_z = (index_z * CZ + cells % CZ).reshape(-1)
    target = ((((index_x * N_GY + index_y) * N_GZ + owners) * OWN_CAP) + index_z * SEND_CAP + slot_index).reshape(-1).astype(jnp.int32)
    blocks = circuit_block.reshape(devices, OWN_CAP)
    update = mna_update.reshape(devices, BLK_DEV, NODES, NODES)
    drive = mna_drive.reshape(devices, BLK_DEV, NODES)
    sense = mna_sense.reshape(devices, BLK_DEV, NODES)
    state = circuit_state.reshape(devices, OWN_CAP, NODES)
    efield = e_field
    hfield = jnp.zeros_like(e_field)
    for iteration in range(ITERS):
        volts = efield[2, glob_x, glob_y, glob_z]
        all_volts = jnp.zeros((devices * OWN_CAP,), jnp.float32).at[target].set(volts).reshape(devices, OWN_CAP)
        state, current = lax.map(lambda group: circuit_step(*group), (state, all_volts, blocks, update, drive, sense))
        port_current = current.reshape(-1)[target]
        upper = jnp.pad(efield, ((0, 0), (0, 1), (0, 1), (0, 1)))
        hfield = hfield - 0.5 * curl_forward(upper)
        lower = jnp.pad(hfield, ((0, 0), (1, 0), (1, 0), (1, 0)))
        source_z = jnp.zeros((NX, NY, NZ), jnp.float32).at[glob_x, glob_y, glob_z].add(port_current)
        source = jnp.stack([jnp.zeros_like(source_z), jnp.zeros_like(source_z), source_z])
        efield = e_keep * efield + e_gain * (curl_backward(lower) - source)
    return efield, hfield, state.reshape(devices * OWN_CAP, NODES)
```

```python
import functools

import jax
import jax.numpy as jnp
from jax import lax
from jax.experimental import pallas as pl
from jax.experimental.pallas import tpu as pltpu
from jax.sharding import PartitionSpec as P

ITERS = 4
MESH = pl.DeviceIdType.MESH
AXES = ("gx", "gy", "gz")
F32 = jnp.float32
BF16 = jnp.bfloat16

MESSAGES = (
    ((1, 0, 0), 0, 3),
    ((-1, 0, 0), 3, 2),
    ((0, 1, 0), 5, 3),
    ((0, -1, 0), 8, 2),
    ((0, 0, 1), 10, 1),
    ((0, 0, -1), 11, 1),
    ((1, -1, 0), 12, 1),
    ((-1, 1, 0), 13, 1),
    ((1, 0, -1), 14, 1),
    ((0, 1, -1), 15, 1),
    ((0, -1, 1), 16, 1),
    ((-1, 0, 1), 17, 1),
)
TILES = 18


def iota(shape, dim):
    return lax.broadcasted_iota(jnp.int32, shape, dim)


def full(row):
    return jnp.broadcast_to(row, (8, 128))


def split(value, parts):
    pieces = []
    for _ in range(parts):
        piece = value.astype(BF16)
        pieces.append(piece)
        value = value - piece.astype(F32)
    return pieces


def dot(a, b):
    return jnp.dot(a, b, preferred_element_type=F32)


def dot_t(a, b):
    return lax.dot_general(a, b, (((1,), (1,)), ((), ())), preferred_element_type=F32)


def kernel(
    sizes,
    e_hbm,
    mat_hbm,
    eps_ref,
    loss_ref,
    cell_ref,
    owner_ref,
    block_ref,
    x_hbm,
    u_hbm,
    d_hbm,
    s_hbm,
    e_out,
    h_out,
    x_out,
    e_ref,
    h_ref,
    mat_ref,
    keep_ref,
    gain_ref,
    hist_ref,
    field_ref,
    x_ref,
    base_ref,
    u_ref,
    d_ref,
    s_ref,
    send_buf,
    recv_buf,
    coef_send,
    coef_recv,
    volt_send,
    volt_recv,
    gather_buf,
    in_sem,
    out_sem,
    send_sem,
    recv_sem,
    coef_ssem,
    coef_rsem,
    volt_ssem,
    volt_rsem,
):
    nz = sizes[2]
    cap = x_ref.shape[0] // nz
    slots = x_ref.shape[0]
    me = [lax.axis_index(a) for a in AXES]

    def exists(offset):
        ok = None
        for at, off, size in zip(me, offset, sizes):
            if off:
                one = at + off >= 0 if off < 0 else at + off < size
                ok = one if ok is None else jnp.logical_and(ok, one)
        return ok

    def device(offset):
        return tuple(at + off for at, off in zip(me, offset))

    def peer(step):
        return lax.rem(me[2] + step, nz)

    loads = [
        pltpu.make_async_copy(src, dst, in_sem.at[n])
        for n, (src, dst) in enumerate(
            (
                (e_hbm, e_ref),
                (mat_hbm, mat_ref),
                (x_hbm, x_ref),
                (u_hbm, u_ref),
                (d_hbm, d_ref),
                (s_hbm, s_ref),
            )
        )
    ]
    for load in loads:
        load.start()
    recv_buf[...] = jnp.zeros(recv_buf.shape, F32)

    barrier = pltpu.get_barrier_semaphore()
    arrivals = jnp.int32(nz - 1)
    for offset, _, _ in MESSAGES:
        if offset[:2] == (0, 0):
            continue
        ok = exists(offset)
        arrivals = arrivals + ok.astype(jnp.int32)

        @pl.when(ok)
        def _(offset=offset):
            pl.semaphore_signal(barrier, inc=1, device_id=device(offset), device_id_type=MESH)

    for step in range(1, nz):
        pl.semaphore_signal(
            barrier, inc=1, device_id=(me[0], me[1], peer(step)), device_id_type=MESH
        )

    row = iota((8, 128), 0)
    lane = iota((8, 128), 1)
    planes = range(8)

    for load in loads[:2]:
        load.wait()
    mat = [mat_ref[i] for i in planes]
    keep = [jnp.zeros((8, 128), F32) for _ in planes]
    gain = [jnp.zeros((8, 128), F32) for _ in planes]
    for m in range(eps_ref.shape[0]):
        loss = jnp.full((8, 128), loss_ref[m], F32)
        eps = jnp.full((8, 128), eps_ref[m], F32)
        keep_m = (1.0 - loss) / (1.0 + loss)
        gain_m = 0.5 / (eps * (1.0 + loss))
        for i in planes:
            same = mat[i] == m
            keep[i] = jnp.where(same, keep_m, keep[i])
            gain[i] = jnp.where(same, gain_m, gain[i])
    for i in planes:
        keep_ref[i] = keep[i]
        gain_ref[i] = gain[i]

    def pack_y(c, j):
        tile = jnp.zeros((8, 128), F32)
        for i in planes:
            tile = jnp.where(row == i, full(e_ref[c, i, j : j + 1, :]), tile)
        return tile

    def pack_z(comps, k):
        tile = jnp.zeros((8, 128), F32)
        for c in comps:
            for i in planes:
                tile = jnp.where(lane == c * 8 + i, full(e_ref[c, i][:, k : k + 1]), tile)
        return tile

    def pack(par):
        y7 = [pack_y(c, 7) for c in range(3)]
        z127 = pack_z((0, 1, 2), 127)
        tiles = [e_ref[c, 7] for c in range(3)]
        tiles += [e_ref[1, 0], e_ref[2, 0]]
        tiles += y7
        tiles += [pack_y(0, 0), pack_y(2, 0)]
        tiles += [z127, pack_z((0, 1), 0)]
        tiles += [pltpu.roll(e_ref[0, 7], 7, 0), pltpu.roll(y7[1], 7, 0)]
        tiles += [pltpu.roll(e_ref[0, 7], 127, 1), pltpu.roll(y7[1], 127, 1)]
        tiles += [pltpu.roll(z127, 7, 0), pltpu.roll(z127, 7, 1)]
        for t, tile in enumerate(tiles):
            send_buf[par, t] = tile

    def message(m, par):
        offset, first, count = MESSAGES[m]
        return pltpu.make_async_remote_copy(
            src_ref=send_buf.at[par, pl.ds(first, count)],
            dst_ref=recv_buf.at[par, pl.ds(first, count)],
            send_sem=send_sem.at[par, m],
            recv_sem=recv_sem.at[par, m],
            device_id=device(offset),
            device_id_type=MESH,
        )

    def send_faces(par):
        for m, (offset, _, _) in enumerate(MESSAGES):

            @pl.when(exists(offset))
            def _(m=m):
                message(m, par).start()

    def wait_faces(par):
        for m, (offset, _, _) in enumerate(MESSAGES):

            @pl.when(exists(tuple(-o for o in offset)))
            def _(m=m):
                message(m, par).wait_recv()

        for m, (offset, _, _) in enumerate(MESSAGES):

            @pl.when(exists(offset))
            def _(m=m):
                message(m, par).wait_send()

    pack(0)

    ports = cell_ref.shape[0]
    owners = [owner_ref[q, 0] for q in range(ports)]
    srow = iota((slots, 128), 0)
    slane = iota((slots, 128), 1)
    slot_cell = jnp.full((slots, 128), -1, jnp.int32)
    lane_cell = jnp.full((8, 128), -1, jnp.int32)
    for q in range(ports):
        index = owners[q] * cap
        for r in range(q):
            index = index + jnp.where(owners[r] == owners[q], 1, 0)
        slot_cell = jnp.where(srow == index, cell_ref[q], slot_cell)
        lane_cell = jnp.where(lax.rem(lane, slots) == index, cell_ref[q], lane_cell)
    in_lane = jnp.logical_and(slot_cell >= 0, (slot_cell & 127) == slane)
    gather = jnp.where((slot_cell >> 7) == lax.rem(slane, 64), 1.0, 0.0).astype(BF16)
    in_row = jnp.broadcast_to((lane_cell >> 7)[0:1, :], (64, 128))
    scatter = jnp.where(in_row == iota((64, 128), 0), 1.0, 0.0).astype(BF16)

    for load in loads[2:]:
        load.wait()
    brow = iota((slots + 8, 128), 0)
    which = jnp.where(brow == slots + 1, 1, 0)
    for s in range(slots):
        which = jnp.where(brow == s, block_ref[s], which)
    first = jnp.concatenate([which, which], axis=1) == 0
    nodes = x_ref.shape[1]
    state = jnp.concatenate(
        [x_ref[...], d_ref[...], jnp.zeros((6, nodes), F32)], axis=0
    )
    sense = jnp.where(
        first,
        jnp.broadcast_to(s_ref[0:1, :], first.shape),
        jnp.broadcast_to(s_ref[1:2, :], first.shape),
    )
    halves = [split(u_ref[b], 2) for b in range(2)]
    drives = [state[slots : slots + 2]]
    readouts = [jnp.sum(state * sense, axis=1, keepdims=True)]
    for n in range(ITERS):
        hi, lo = split(state, 2)
        both = [
            dot_t(hi, high) + (dot_t(hi, low) + dot_t(lo, high)) for high, low in halves
        ]
        state = jnp.where(first, both[0], both[1])
        readouts.append(jnp.sum(state * sense, axis=1, keepdims=True))
        if n < ITERS - 1:
            drives.append(state[slots : slots + 2])
    base_ref[...] = state[:slots]
    is_first = first[:slots, :128]
    coefs = jnp.zeros((slots, 128), F32)
    for n in range(ITERS):
        coefs = jnp.where(slane == n, readouts[n + 1][:slots], coefs)
        kick = jnp.where(is_first, readouts[n][slots : slots + 1], readouts[n][slots + 1 : slots + 2])
        coefs = jnp.where(slane == ITERS + n, kick, coefs)
    for g in range(nz):
        coef_send[g] = coefs[g * cap : (g + 1) * cap]

    pl.semaphore_wait(barrier, arrivals)

    send_faces(0)

    def exchange(step, src, dst, ssem, rsem):
        there = peer(step)
        return pltpu.make_async_remote_copy(
            src_ref=src.at[there],
            dst_ref=dst.at[me[2]],
            send_sem=ssem.at[step],
            recv_sem=rsem.at[step],
            device_id=(me[0], me[1], there),
            device_id_type=MESH,
        )

    coef_copies = [
        exchange(step, coef_send, coef_recv, coef_ssem, coef_rsem) for step in range(1, nz)
    ]
    for copy in coef_copies:
        copy.start()
    coef_recv[me[2]] = coef_send[me[2]]

    low = [jnp.where(me[d] > 0, 1.0, 0.0).astype(F32) for d in range(3)]
    ghosts = None
    volts = []

    for n in range(ITERS):
        par = n % 2
        e_z = [e_ref[2, i] for i in planes]
        for i in planes:
            hist_ref[n, i] = e_z[i]
        stack = jnp.concatenate(e_z, axis=0)
        found = dot(gather, jnp.concatenate(split(stack, 2), axis=0))
        volts.append(
            jnp.sum(jnp.where(in_lane, found, 0.0), axis=1, keepdims=True)
        )
        if n == ITERS - 1:
            tile = jnp.zeros((slots, 128), F32)
            for k in range(ITERS):
                tile = jnp.where(slane == k, volts[k], tile)
            for g in range(nz):
                volt_send[g] = tile[g * cap : (g + 1) * cap]
            volt_copies = [
                exchange(step, volt_send, volt_recv, volt_ssem, volt_rsem)
                for step in range(1, nz)
            ]
            for copy in volt_copies:
                copy.start()
            volt_recv[me[2]] = volt_send[me[2]]

        wait_faces(par)

        def got(t, par=par):
            return recv_buf[par, t]

        ex_m, ey_m, ez_m = got(0), got(1), got(2)
        ex_k = jnp.where(lane == 127, got(14), pltpu.roll(ex_m, 127, 1))
        ex_j = jnp.where(row == 7, got(12), pltpu.roll(ex_m, 7, 0))
        hy_x = -0.5 * ((ex_k - ex_m) - (e_ref[2, 0] - ez_m))
        hz_x = -0.5 * ((e_ref[1, 0] - ey_m) - (ex_j - ex_m))
        fx_m, fy_m, fz_m = got(5), got(6), got(7)
        fx_0, fz_0 = send_buf[par, 8], send_buf[par, 9]
        fy_k = jnp.where(lane == 127, got(15), pltpu.roll(fy_m, 127, 1))
        fy_i = jnp.where(row == 7, got(13), pltpu.roll(fy_m, 7, 0))
        hx_y = -0.5 * ((fz_0 - fz_m) - (fy_k - fy_m))
        hz_y = -0.5 * ((fy_i - fy_m) - (fx_0 - fx_m))
        g_m, g_0 = got(10), send_buf[par, 11]
        gz_j = jnp.where(row == 7, got(16), pltpu.roll(g_m, 7, 0)) - g_m
        gz_i = jnp.where(lane == 23, got(17), pltpu.roll(g_m, 127, 1)) - g_m
        g_d = g_0 - g_m
        h_z = -0.5 * jnp.where(
            lane < 8, g_d - pltpu.roll(gz_i, 128 - 16, 1), pltpu.roll(gz_j, 128 - 8, 1) - g_d
        )
        new = [hy_x * low[0], hz_x * low[0], hx_y * low[1], hz_y * low[1], h_z * low[2]]
        ghosts = new if ghosts is None else [a + b for a, b in zip(ghosts, new)]
        hy_x, hz_x, hx_y, hz_y, h_z = ghosts

        zp = got(11)
        for i in planes:
            ex, ey, ez = e_ref[0, i], e_ref[1, i], e_ref[2, i]
            ex_j = jnp.where(row == 7, full(recv_buf[par, 8, i : i + 1, :]), pltpu.roll(ex, 7, 0))
            ez_j = jnp.where(row == 7, full(recv_buf[par, 9, i : i + 1, :]), pltpu.roll(ez, 7, 0))
            ex_k = jnp.where(lane == 127, full(zp[:, i : i + 1]), pltpu.roll(ex, 127, 1))
            ey_k = jnp.where(lane == 127, full(zp[:, 8 + i : 9 + i]), pltpu.roll(ey, 127, 1))
            ey_i = e_ref[1, i + 1] if i < 7 else got(3)
            ez_i = e_ref[2, i + 1] if i < 7 else got(4)
            hx = -0.5 * ((ez_j - ez) - (ey_k - ey))
            hy = -0.5 * ((ex_k - ex) - (ez_i - ez))
            hz = -0.5 * ((ey_i - ey) - (ex_j - ex))
            for c, value in enumerate((hx, hy, hz)):
                h_ref[c, i] = value if n == 0 else h_ref[c, i] + value

        if n == 0:
            for copy in coef_copies:
                copy.wait_recv()
            for copy in coef_copies:
                copy.wait_send()
            for g in range(nz):
                gather_buf[g * cap : (g + 1) * cap, :] = coef_recv[g]
            table = gather_buf[...]
            spread = jnp.concatenate(
                [
                    jnp.where(in_lane, jnp.broadcast_to(table[:, k : k + 1], (slots, 128)), 0.0)
                    for k in range(2 * ITERS)
                ],
                axis=1,
            )
            pieces = split(spread, 3) + [jnp.zeros(spread.shape, BF16)]
            field_ref[...] = dot(scatter, jnp.concatenate(pieces, axis=0))

        for i in planes:
            hx, hy, hz = h_ref[0, i], h_ref[1, i], h_ref[2, i]
            hx_j = jnp.where(row == 0, full(hx_y[i : i + 1, :]), pltpu.roll(hx, 1, 0))
            hz_j = jnp.where(row == 0, full(hz_y[i : i + 1, :]), pltpu.roll(hz, 1, 0))
            hy_k = jnp.where(lane == 0, full(h_z[:, i : i + 1]), pltpu.roll(hy, 1, 1))
            hx_k = jnp.where(lane == 0, full(h_z[:, 8 + i : 9 + i]), pltpu.roll(hx, 1, 1))
            hy_i = h_ref[1, i - 1] if i > 0 else hy_x
            hz_i = h_ref[2, i - 1] if i > 0 else hz_x
            rows = slice(8 * i, 8 * i + 8)
            current = field_ref[rows, 128 * n : 128 * (n + 1)]
            for k in range(n + 1):
                at = ITERS + n - k
                current = current + field_ref[rows, 128 * at : 128 * (at + 1)] * hist_ref[k, i]
            keep, gain = keep_ref[i], gain_ref[i]
            e_ref[0, i] = keep * e_ref[0, i] + gain * ((hz - hz_j) - (hy - hy_k))
            e_ref[1, i] = keep * e_ref[1, i] + gain * ((hx - hx_k) - (hz - hz_i))
            e_ref[2, i] = keep * e_ref[2, i] + gain * (((hy - hy_i) - (hx - hx_j)) - current)

        if n < ITERS - 1:
            pack(1 - par)
            send_faces(1 - par)

    stores = [
        pltpu.make_async_copy(e_ref, e_out, out_sem.at[0]),
        pltpu.make_async_copy(h_ref, h_out, out_sem.at[1]),
        pltpu.make_async_copy(base_ref, x_out, out_sem.at[2]),
    ]
    stores[0].start()
    stores[1].start()

    for copy in volt_copies:
        copy.wait_recv()
    for copy in volt_copies:
        copy.wait_send()
    for g in range(nz):
        gather_buf[g * cap : (g + 1) * cap, :] = volt_recv[g]
    table = gather_buf[...]
    final = base_ref[...]
    pick = first[:slots]
    for k in range(ITERS):
        drive = drives[ITERS - 1 - k]
        rows = jnp.where(
            pick,
            jnp.broadcast_to(drive[0:1], final.shape),
            jnp.broadcast_to(drive[1:2], final.shape),
        )
        final = final + rows * table[:, k : k + 1]
    base_ref[...] = final
    stores[2].start()
    for store in stores:
        store.wait()


def solution(mesh):
    sizes = tuple(mesh.shape[a] for a in AXES)

    def local(
        e_field,
        material,
        permittivity,
        loss,
        port_cell,
        port_owner,
        circuit_block,
        circuit_state,
        mna_update,
        mna_drive,
        mna_sense,
    ):
        slots, nodes = circuit_state.shape
        cap = slots // sizes[2]
        anywhere = pl.BlockSpec(memory_space=pl.ANY)
        scalars = pl.BlockSpec(memory_space=pltpu.SMEM)
        dma = pltpu.SemaphoreType.DMA
        return pl.pallas_call(
            functools.partial(kernel, sizes),
            out_shape=[
                jax.ShapeDtypeStruct(e_field.shape, F32),
                jax.ShapeDtypeStruct(e_field.shape, F32),
                jax.ShapeDtypeStruct(circuit_state.shape, F32),
            ],
            in_specs=[anywhere] * 2 + [scalars] * 5 + [anywhere] * 4,
            out_specs=[anywhere] * 3,
            scratch_shapes=[
                pltpu.VMEM(e_field.shape, F32),
                pltpu.VMEM(e_field.shape, F32),
                pltpu.VMEM(material.shape, jnp.int32),
                pltpu.VMEM(material.shape, F32),
                pltpu.VMEM(material.shape, F32),
                pltpu.VMEM((ITERS,) + material.shape, F32),
                pltpu.VMEM((64, 2 * ITERS * 128), F32),
                pltpu.VMEM(circuit_state.shape, F32),
                pltpu.VMEM(circuit_state.shape, F32),
                pltpu.VMEM(mna_update.shape, F32),
                pltpu.VMEM(mna_drive.shape, F32),
                pltpu.VMEM(mna_sense.shape, F32),
                pltpu.VMEM((2, TILES, 8, 128), F32),
                pltpu.VMEM((2, TILES, 8, 128), F32),
                pltpu.VMEM((sizes[2], cap, 128), F32),
                pltpu.VMEM((sizes[2], cap, 128), F32),
                pltpu.VMEM((sizes[2], cap, 128), F32),
                pltpu.VMEM((sizes[2], cap, 128), F32),
                pltpu.VMEM((slots, 128), F32),
                dma((6,)),
                dma((3,)),
                dma((2, len(MESSAGES))),
                dma((2, len(MESSAGES))),
                dma((sizes[2],)),
                dma((sizes[2],)),
                dma((sizes[2],)),
                dma((sizes[2],)),
            ],
            compiler_params=pltpu.CompilerParams(
                collective_id=0, has_side_effects=True, vmem_limit_bytes=32 * 1024 * 1024
            ),
        )(
            e_field,
            material,
            permittivity,
            loss,
            port_cell,
            port_owner,
            circuit_block,
            circuit_state,
            mna_update,
            mna_drive,
            mna_sense,
        )

    placed = (
        P(None, "gx", "gy", "gz"),
        P("gx", "gy", "gz"),
        P(),
        P(),
        P(("gx", "gy", "gz")),
        P(("gx", "gy", "gz"), None),
        P(("gx", "gy", "gz")),
        P(("gx", "gy", "gz"), None),
        P(("gx", "gy", "gz"), None, None),
        P(("gx", "gy", "gz"), None),
        P(("gx", "gy", "gz"), None),
    )
    return jax.shard_map(
        local,
        mesh=mesh,
        in_specs=placed,
        out_specs=(
            P(None, "gx", "gy", "gz"),
            P(None, "gx", "gy", "gz"),
            P(("gx", "gy", "gz"), None),
        ),
        check_vma=False,
    )
```

```python
import functools

import jax
import jax.numpy as jnp
from jax import lax
from jax.experimental import pallas as pl
from jax.experimental.pallas import tpu as pltpu
from jax.sharding import PartitionSpec as P

ITERS = 4
MESH = pl.DeviceIdType.MESH
AXES = ("gx", "gy", "gz")
F32 = jnp.float32
BF16 = jnp.bfloat16

MESSAGES = (
    ((1, 0, -1), 14, 1),
    ((-1, 0, 1), 17, 1),
    ((1, -1, 0), 12, 1),
    ((-1, 1, 0), 13, 1),
    ((1, 0, 0), 0, 3),
    ((-1, 0, 0), 3, 2),
    ((0, -1, 1), 16, 1),
    ((0, 1, -1), 15, 1),
    ((0, 0, 1), 10, 1),
    ((0, 0, -1), 11, 1),
    ((0, 1, 0), 5, 3),
    ((0, -1, 0), 8, 2),
)
TILES = 18


def iota(shape, dim):
    return lax.broadcasted_iota(jnp.int32, shape, dim)


def full(row):
    return jnp.broadcast_to(row, (8, 128))


def split(value, parts):
    pieces = []
    for _ in range(parts):
        piece = value.astype(BF16)
        pieces.append(piece)
        value = value - piece.astype(F32)
    return pieces


def dot(a, b):
    return jnp.dot(a, b, preferred_element_type=F32)


def dot_t(a, b):
    return lax.dot_general(a, b, (((1,), (1,)), ((), ())), preferred_element_type=F32)


def kernel(
    sizes,
    e_hbm,
    mat_hbm,
    eps_hbm,
    loss_hbm,
    cell_hbm,
    owner_hbm,
    block_hbm,
    x_hbm,
    u_hbm,
    d_hbm,
    s_hbm,
    e_ref,
    h_ref,
    base_ref,
    eps_ref,
    loss_ref,
    cell_ref,
    owner_ref,
    block_ref,
    mat_ref,
    keep_ref,
    gain_ref,
    hist_ref,
    field_ref,
    x_ref,
    u_ref,
    d_ref,
    s_ref,
    send_buf,
    recv_buf,
    coef_send,
    coef_recv,
    volt_send,
    volt_recv,
    gather_buf,
    in_sem,
    send_sem,
    recv_sem,
    coef_ssem,
    coef_rsem,
    volt_ssem,
    volt_rsem,
):
    nz = sizes[2]
    cap = x_ref.shape[0] // nz
    slots = x_ref.shape[0]
    me = [lax.axis_index(a) for a in AXES]

    def exists(offset):
        ok = None
        for at, off, size in zip(me, offset, sizes):
            if off:
                one = at + off >= 0 if off < 0 else at + off < size
                ok = one if ok is None else jnp.logical_and(ok, one)
        return ok

    def device(offset):
        return tuple(at + off for at, off in zip(me, offset))

    def peer(step):
        return lax.rem(me[2] + step, nz)

    loads = [
        pltpu.make_async_copy(src, dst, in_sem.at[n])
        for n, (src, dst) in enumerate(
            (
                (e_hbm, e_ref),
                (mat_hbm, mat_ref),
                (eps_hbm, eps_ref),
                (loss_hbm, loss_ref),
                (cell_hbm, cell_ref),
                (owner_hbm, owner_ref),
                (block_hbm, block_ref),
                (u_hbm, u_ref),
                (x_hbm, x_ref),
                (d_hbm, d_ref),
                (s_hbm, s_ref),
            )
        )
    ]

    recv_buf[...] = jnp.zeros(recv_buf.shape, F32)

    barrier = pltpu.get_barrier_semaphore()
    arrivals = jnp.int32(nz - 1)
    for offset, _, _ in MESSAGES:
        if offset[:2] == (0, 0):
            continue
        ok = exists(offset)
        arrivals = arrivals + ok.astype(jnp.int32)

        @pl.when(ok)
        def _(offset=offset):
            pl.semaphore_signal(barrier, inc=1, device_id=device(offset), device_id_type=MESH)

    for step in range(1, nz):
        pl.semaphore_signal(
            barrier, inc=1, device_id=(me[0], me[1], peer(step)), device_id_type=MESH
        )

    for load in loads:
        load.start()

    row = iota((8, 128), 0)
    lane = iota((8, 128), 1)
    planes = range(8)

    for load in loads[1:7]:
        load.wait()
    mat = [mat_ref[i] for i in planes]
    keep = [jnp.zeros((8, 128), F32) for _ in planes]
    gain = [jnp.zeros((8, 128), F32) for _ in planes]
    for m in range(eps_ref.shape[0]):
        loss = jnp.full((8, 128), loss_ref[m], F32)
        eps = jnp.full((8, 128), eps_ref[m], F32)
        keep_m = (1.0 - loss) / (1.0 + loss)
        gain_m = 0.5 / (eps * (1.0 + loss))
        for i in planes:
            same = mat[i] == m
            keep[i] = jnp.where(same, keep_m, keep[i])
            gain[i] = jnp.where(same, gain_m, gain[i])
    for i in planes:
        keep_ref[i] = keep[i]
        gain_ref[i] = gain[i]

    def pack_y(c, j):
        tile = jnp.zeros((8, 128), F32)
        for i in planes:
            tile = jnp.where(row == i, full(e_ref[c, i, j : j + 1, :]), tile)
        return tile

    def pack_z(comps, k):
        tile = jnp.zeros((8, 128), F32)
        for c in comps:
            for i in planes:
                tile = jnp.where(lane == c * 8 + i, full(e_ref[c, i][:, k : k + 1]), tile)
        return tile

    def pack(par):
        y7 = [pack_y(c, 7) for c in range(3)]
        z127 = pack_z((0, 1, 2), 127)
        tiles = [e_ref[c, 7] for c in range(3)]
        tiles += [e_ref[1, 0], e_ref[2, 0]]
        tiles += y7
        tiles += [pack_y(0, 0), pack_y(2, 0)]
        tiles += [z127, pack_z((0, 1), 0)]
        tiles += [pltpu.roll(e_ref[0, 7], 7, 0), pltpu.roll(y7[1], 7, 0)]
        tiles += [pltpu.roll(e_ref[0, 7], 127, 1), pltpu.roll(y7[1], 127, 1)]
        tiles += [pltpu.roll(z127, 7, 0), pltpu.roll(z127, 7, 1)]
        for t, tile in enumerate(tiles):
            send_buf[par, t] = tile

    def message(m, par):
        offset, first, count = MESSAGES[m]
        return pltpu.make_async_remote_copy(
            src_ref=send_buf.at[par, pl.ds(first, count)],
            dst_ref=recv_buf.at[par, pl.ds(first, count)],
            send_sem=send_sem.at[par, m],
            recv_sem=recv_sem.at[par, m],
            device_id=device(offset),
            device_id_type=MESH,
        )

    def send_faces(par):
        for m, (offset, _, _) in enumerate(MESSAGES):

            @pl.when(exists(offset))
            def _(m=m):
                message(m, par).start()

    def wait_faces(par):
        for m, (offset, _, _) in enumerate(MESSAGES):

            @pl.when(exists(tuple(-o for o in offset)))
            def _(m=m):
                message(m, par).wait_recv()

        for m, (offset, _, _) in enumerate(MESSAGES):

            @pl.when(exists(offset))
            def _(m=m):
                message(m, par).wait_send()

    loads[0].wait()
    pack(0)

    ports = cell_ref.shape[0]
    owners = [owner_ref[q] for q in range(ports)]
    srow = iota((slots, 128), 0)
    slane = iota((slots, 128), 1)
    slot_cell = jnp.full((slots, 128), -1, jnp.int32)
    lane_cell = jnp.full((8, 128), -1, jnp.int32)
    for q in range(ports):
        index = owners[q] * cap
        for r in range(q):
            index = index + jnp.where(owners[r] == owners[q], 1, 0)
        slot_cell = jnp.where(srow == index, cell_ref[q], slot_cell)
        lane_cell = jnp.where(lax.rem(lane, slots) == index, cell_ref[q], lane_cell)
    in_lane = jnp.logical_and(slot_cell >= 0, (slot_cell & 127) == slane)
    gather = jnp.where((slot_cell >> 7) == lax.rem(slane, 64), 1.0, 0.0).astype(BF16)
    in_row = jnp.broadcast_to((lane_cell >> 7)[0:1, :], (64, 128))
    scatter = jnp.where(in_row == iota((64, 128), 0), 1.0, 0.0).astype(BF16)

    for load in loads[7:]:
        load.wait()
    brow = iota((slots + 8, 128), 0)
    which = jnp.where(brow == slots + 1, 1, 0)
    for s in range(slots):
        which = jnp.where(brow == s, block_ref[s], which)
    first = jnp.concatenate([which, which], axis=1) == 0
    nodes = x_ref.shape[1]
    state = jnp.concatenate(
        [x_ref[...], d_ref[...], jnp.zeros((6, nodes), F32)], axis=0
    )
    sense = jnp.where(
        first,
        jnp.broadcast_to(s_ref[0:1, :], first.shape),
        jnp.broadcast_to(s_ref[1:2, :], first.shape),
    )
    halves = [split(u_ref[b], 2) for b in range(2)]
    drives = [state[slots : slots + 2]]
    readouts = [jnp.sum(state * sense, axis=1, keepdims=True)]
    for n in range(ITERS):
        hi, lo = split(state, 2)
        both = [
            dot_t(hi, high) + (dot_t(hi, low) + dot_t(lo, high)) for high, low in halves
        ]
        state = jnp.where(first, both[0], both[1])
        readouts.append(jnp.sum(state * sense, axis=1, keepdims=True))
        if n < ITERS - 1:
            drives.append(state[slots : slots + 2])
    base_ref[...] = state[:slots]
    is_first = first[:slots, :128]
    coefs = jnp.zeros((slots, 128), F32)
    for n in range(ITERS):
        coefs = jnp.where(slane == n, readouts[n + 1][:slots], coefs)
        kick = jnp.where(is_first, readouts[n][slots : slots + 1], readouts[n][slots + 1 : slots + 2])
        coefs = jnp.where(slane == ITERS + n, kick, coefs)
    for g in range(nz):
        coef_send[g] = coefs[g * cap : (g + 1) * cap]

    pl.semaphore_wait(barrier, arrivals)

    send_faces(0)

    def exchange(step, src, dst, ssem, rsem):
        there = peer(step)
        return pltpu.make_async_remote_copy(
            src_ref=src.at[there],
            dst_ref=dst.at[me[2]],
            send_sem=ssem.at[step],
            recv_sem=rsem.at[step],
            device_id=(me[0], me[1], there),
            device_id_type=MESH,
        )

    coef_copies = [
        exchange(step, coef_send, coef_recv, coef_ssem, coef_rsem) for step in range(1, nz)
    ]
    for copy in coef_copies:
        copy.start()
    coef_recv[me[2]] = coef_send[me[2]]

    low = [jnp.where(me[d] > 0, 1.0, 0.0).astype(F32) for d in range(3)]
    ghosts = None
    volts = []

    for n in range(ITERS):
        par = n % 2
        e_z = [e_ref[2, i] for i in planes]
        for i in planes:
            hist_ref[n, i] = e_z[i]
        stack = jnp.concatenate(e_z, axis=0)
        found = dot(gather, jnp.concatenate(split(stack, 2), axis=0))
        volts.append(
            jnp.sum(jnp.where(in_lane, found, 0.0), axis=1, keepdims=True)
        )
        if n == ITERS - 1:
            tile = jnp.zeros((slots, 128), F32)
            for k in range(ITERS):
                tile = jnp.where(slane == k, volts[k], tile)
            for g in range(nz):
                volt_send[g] = tile[g * cap : (g + 1) * cap]
            volt_copies = [
                exchange(step, volt_send, volt_recv, volt_ssem, volt_rsem)
                for step in range(1, nz)
            ]
            for copy in volt_copies:
                copy.start()
            volt_recv[me[2]] = volt_send[me[2]]

        wait_faces(par)

        def got(t, par=par):
            return recv_buf[par, t]

        ex_m, ey_m, ez_m = got(0), got(1), got(2)
        ex_k = jnp.where(lane == 127, got(14), pltpu.roll(ex_m, 127, 1))
        ex_j = jnp.where(row == 7, got(12), pltpu.roll(ex_m, 7, 0))
        hy_x = -0.5 * ((ex_k - ex_m) - (e_ref[2, 0] - ez_m))
        hz_x = -0.5 * ((e_ref[1, 0] - ey_m) - (ex_j - ex_m))
        fx_m, fy_m, fz_m = got(5), got(6), got(7)
        fx_0, fz_0 = send_buf[par, 8], send_buf[par, 9]
        fy_k = jnp.where(lane == 127, got(15), pltpu.roll(fy_m, 127, 1))
        fy_i = jnp.where(row == 7, got(13), pltpu.roll(fy_m, 7, 0))
        hx_y = -0.5 * ((fz_0 - fz_m) - (fy_k - fy_m))
        hz_y = -0.5 * ((fy_i - fy_m) - (fx_0 - fx_m))
        g_m, g_0 = got(10), send_buf[par, 11]
        gz_j = jnp.where(row == 7, got(16), pltpu.roll(g_m, 7, 0)) - g_m
        gz_i = jnp.where(lane == 23, got(17), pltpu.roll(g_m, 127, 1)) - g_m
        g_d = g_0 - g_m
        h_z = -0.5 * jnp.where(
            lane < 8, g_d - pltpu.roll(gz_i, 128 - 16, 1), pltpu.roll(gz_j, 128 - 8, 1) - g_d
        )
        new = [hy_x * low[0], hz_x * low[0], hx_y * low[1], hz_y * low[1], h_z * low[2]]
        ghosts = new if ghosts is None else [a + b for a, b in zip(ghosts, new)]
        hy_x, hz_x, hx_y, hz_y, h_z = ghosts

        zp = got(11)
        for i in planes:
            ex, ey, ez = e_ref[0, i], e_ref[1, i], e_ref[2, i]
            ex_j = jnp.where(row == 7, full(recv_buf[par, 8, i : i + 1, :]), pltpu.roll(ex, 7, 0))
            ez_j = jnp.where(row == 7, full(recv_buf[par, 9, i : i + 1, :]), pltpu.roll(ez, 7, 0))
            ex_k = jnp.where(lane == 127, full(zp[:, i : i + 1]), pltpu.roll(ex, 127, 1))
            ey_k = jnp.where(lane == 127, full(zp[:, 8 + i : 9 + i]), pltpu.roll(ey, 127, 1))
            ey_i = e_ref[1, i + 1] if i < 7 else got(3)
            ez_i = e_ref[2, i + 1] if i < 7 else got(4)
            hx = -0.5 * ((ez_j - ez) - (ey_k - ey))
            hy = -0.5 * ((ex_k - ex) - (ez_i - ez))
            hz = -0.5 * ((ey_i - ey) - (ex_j - ex))
            for c, value in enumerate((hx, hy, hz)):
                h_ref[c, i] = value if n == 0 else h_ref[c, i] + value

        if n == 0:
            for copy in coef_copies:
                copy.wait_recv()
            for copy in coef_copies:
                copy.wait_send()
            for g in range(nz):
                gather_buf[g * cap : (g + 1) * cap, :] = coef_recv[g]
            table = gather_buf[...]
            spread = jnp.concatenate(
                [
                    jnp.where(in_lane, jnp.broadcast_to(table[:, k : k + 1], (slots, 128)), 0.0)
                    for k in range(2 * ITERS)
                ],
                axis=1,
            )
            pieces = split(spread, 3) + [jnp.zeros(spread.shape, BF16)]
            field_ref[...] = dot(scatter, jnp.concatenate(pieces, axis=0))

        for i in planes:
            hx, hy, hz = h_ref[0, i], h_ref[1, i], h_ref[2, i]
            hx_j = jnp.where(row == 0, full(hx_y[i : i + 1, :]), pltpu.roll(hx, 1, 0))
            hz_j = jnp.where(row == 0, full(hz_y[i : i + 1, :]), pltpu.roll(hz, 1, 0))
            hy_k = jnp.where(lane == 0, full(h_z[:, i : i + 1]), pltpu.roll(hy, 1, 1))
            hx_k = jnp.where(lane == 0, full(h_z[:, 8 + i : 9 + i]), pltpu.roll(hx, 1, 1))
            hy_i = h_ref[1, i - 1] if i > 0 else hy_x
            hz_i = h_ref[2, i - 1] if i > 0 else hz_x
            rows = slice(8 * i, 8 * i + 8)
            current = field_ref[rows, 128 * n : 128 * (n + 1)]
            for k in range(n + 1):
                at = ITERS + n - k
                current = current + field_ref[rows, 128 * at : 128 * (at + 1)] * hist_ref[k, i]
            keep, gain = keep_ref[i], gain_ref[i]
            e_ref[0, i] = keep * e_ref[0, i] + gain * ((hz - hz_j) - (hy - hy_k))
            e_ref[1, i] = keep * e_ref[1, i] + gain * ((hx - hx_k) - (hz - hz_i))
            e_ref[2, i] = keep * e_ref[2, i] + gain * (((hy - hy_i) - (hx - hx_j)) - current)

        if n < ITERS - 1:
            pack(1 - par)
            send_faces(1 - par)

    for copy in volt_copies:
        copy.wait_recv()
    for copy in volt_copies:
        copy.wait_send()
    for g in range(nz):
        gather_buf[g * cap : (g + 1) * cap, :] = volt_recv[g]
    table = gather_buf[...]
    final = base_ref[...]
    pick = first[:slots]
    for k in range(ITERS):
        drive = drives[ITERS - 1 - k]
        rows = jnp.where(
            pick,
            jnp.broadcast_to(drive[0:1], final.shape),
            jnp.broadcast_to(drive[1:2], final.shape),
        )
        final = final + rows * table[:, k : k + 1]
    base_ref[...] = final


def hand_out(*refs):
    sources, results, sem = refs[:3], refs[3:6], refs[6]
    copies = [
        pltpu.make_async_copy(src, dst, sem.at[n])
        for n, (src, dst) in enumerate(zip(sources, results))
    ]
    for copy in copies:
        copy.start()
    for copy in copies:
        copy.wait()


def solution(mesh):
    sizes = tuple(mesh.shape[a] for a in AXES)

    def local(
        e_field,
        material,
        permittivity,
        loss,
        port_cell,
        port_owner,
        circuit_block,
        circuit_state,
        mna_update,
        mna_drive,
        mna_sense,
    ):
        slots, nodes = circuit_state.shape
        cap = slots // sizes[2]
        hbm = pl.BlockSpec(memory_space=pltpu.HBM)
        dma = pltpu.SemaphoreType.DMA
        vmem = pl.BlockSpec(memory_space=pltpu.VMEM)
        shapes = (e_field.shape, e_field.shape, circuit_state.shape)
        results = pl.pallas_call(
            functools.partial(kernel, sizes),
            out_shape=[pltpu.VMEM(shape, F32) for shape in shapes],
            in_specs=[hbm] * 11,
            out_specs=[vmem] * 3,
            scratch_shapes=[
                pltpu.SMEM(permittivity.shape, F32),
                pltpu.SMEM(loss.shape, F32),
                pltpu.SMEM(port_cell.shape, jnp.int32),
                pltpu.SMEM(port_cell.shape, jnp.int32),
                pltpu.SMEM(circuit_block.shape, jnp.int32),
                pltpu.VMEM(material.shape, jnp.int32),
                pltpu.VMEM(material.shape, F32),
                pltpu.VMEM(material.shape, F32),
                pltpu.VMEM((ITERS,) + material.shape, F32),
                pltpu.VMEM((64, 2 * ITERS * 128), F32),
                pltpu.VMEM(circuit_state.shape, F32),
                pltpu.VMEM(mna_update.shape, F32),
                pltpu.VMEM(mna_drive.shape, F32),
                pltpu.VMEM(mna_sense.shape, F32),
                pltpu.VMEM((2, TILES, 8, 128), F32),
                pltpu.VMEM((2, TILES, 8, 128), F32),
                pltpu.VMEM((sizes[2], cap, 128), F32),
                pltpu.VMEM((sizes[2], cap, 128), F32),
                pltpu.VMEM((sizes[2], cap, 128), F32),
                pltpu.VMEM((sizes[2], cap, 128), F32),
                pltpu.VMEM((slots, 128), F32),
                dma((11,)),
                dma((2, len(MESSAGES))),
                dma((2, len(MESSAGES))),
                dma((sizes[2],)),
                dma((sizes[2],)),
                dma((sizes[2],)),
                dma((sizes[2],)),
            ],
            compiler_params=pltpu.CompilerParams(
                collective_id=0, has_side_effects=True, vmem_limit_bytes=32 * 1024 * 1024
            ),
        )(
            *(
                pltpu.with_memory_space_constraint(array, pltpu.HBM)
                for array in (
                    e_field,
                    material,
                    permittivity,
                    loss,
                    port_cell,
                    port_owner.reshape(-1),
                    circuit_block,
                    circuit_state,
                    mna_update,
                    mna_drive,
                    mna_sense,
                )
            )
        )
        return pl.pallas_call(
            hand_out,
            out_shape=[jax.ShapeDtypeStruct(shape, F32) for shape in shapes],
            in_specs=[vmem] * 3,
            out_specs=[hbm] * 3,
            scratch_shapes=[dma((3,))],
        )(*(pltpu.with_memory_space_constraint(r, pltpu.VMEM) for r in results))

    placed = (
        P(None, "gx", "gy", "gz"),
        P("gx", "gy", "gz"),
        P(),
        P(),
        P(("gx", "gy", "gz")),
        P(("gx", "gy", "gz"), None),
        P(("gx", "gy", "gz")),
        P(("gx", "gy", "gz"), None),
        P(("gx", "gy", "gz"), None, None),
        P(("gx", "gy", "gz"), None),
        P(("gx", "gy", "gz"), None),
    )
    return jax.shard_map(
        local,
        mesh=mesh,
        in_specs=placed,
        out_specs=(
            P(None, "gx", "gy", "gz"),
            P(None, "gx", "gy", "gz"),
            P(("gx", "gy", "gz"), None),
        ),
        check_vma=False,
    )
```

```python
import functools

import jax
import jax.numpy as jnp
from jax import lax
from jax.experimental import pallas as pl
from jax.experimental.pallas import tpu as pltpu
from jax.sharding import PartitionSpec as P

ITERS = 4
MESH = pl.DeviceIdType.MESH
AXES = ("gx", "gy", "gz")
F32 = jnp.float32
BF16 = jnp.bfloat16

MESSAGES = (
    ((1, 0, -1), 0, 1, 1),
    ((-1, 0, 1), 2, 1, 1),
    ((1, 0, 0), 4, 3, 1),
    ((-1, 0, 0), 8, 2, 1),
    ((1, -1, 0), 11, 1, 1),
    ((-1, 1, 0), 13, 1, 0),
    ((0, -1, 1), 14, 1, 0),
    ((0, 1, -1), 15, 1, 0),
    ((0, 0, 1), 16, 1, 0),
    ((0, 0, -1), 17, 1, 0),
    ((0, 1, 0), 18, 3, 0),
    ((0, -1, 0), 21, 2, 0),
)
TILES = 23
LATE = (0, 1)
FAR = range(6)
NEAR = range(6, 12)

def iota(shape, dim):
    return lax.broadcasted_iota(jnp.int32, shape, dim)


def full(row):
    return jnp.broadcast_to(row, (8, 128))


def split(value, parts):
    pieces = []
    for _ in range(parts):
        piece = value.astype(BF16)
        pieces.append(piece)
        value = value - piece.astype(F32)
    return pieces


def dot(a, b):
    return jnp.dot(a, b, preferred_element_type=F32)


def dot_t(a, b):
    return lax.dot_general(a, b, (((1,), (1,)), ((), ())), preferred_element_type=F32)


def kernel(
    sizes,
    e_hbm,
    mat_hbm,
    eps_hbm,
    loss_hbm,
    cell_hbm,
    owner_hbm,
    block_hbm,
    x_hbm,
    u_hbm,
    d_hbm,
    s_hbm,
    e_ref,
    h_ref,
    base_ref,
    eps_ref,
    loss_ref,
    cell_ref,
    owner_ref,
    block_ref,
    mat_ref,
    keep_ref,
    gain_ref,
    hist_ref,
    field_ref,
    x_ref,
    u_ref,
    d_ref,
    s_ref,
    send_buf,
    recv_buf,
    coef_send,
    coef_recv,
    volt_send,
    volt_recv,
    gather_buf,
    in_sem,
    send_sem,
    recv_sem,
    coef_ssem,
    coef_rsem,
    volt_ssem,
    volt_rsem,
):
    nz = sizes[2]
    cap = x_ref.shape[0] // nz
    slots = x_ref.shape[0]
    me = [lax.axis_index(a) for a in AXES]

    def exists(offset):
        ok = None
        for at, off, size in zip(me, offset, sizes):
            if off:
                one = at + off >= 0 if off < 0 else at + off < size
                ok = one if ok is None else jnp.logical_and(ok, one)
        return ok

    def device(offset):
        return tuple(at + off for at, off in zip(me, offset))

    def peer(step):
        return lax.rem(me[2] + step, nz)

    loads = [
        pltpu.make_async_copy(src, dst, in_sem.at[n])
        for n, (src, dst) in enumerate(
            (
                (e_hbm, e_ref),
                (mat_hbm, mat_ref),
                (eps_hbm, eps_ref),
                (loss_hbm, loss_ref),
                (cell_hbm, cell_ref),
                (owner_hbm, owner_ref),
                (block_hbm, block_ref),
                (u_hbm, u_ref),
                (x_hbm, x_ref),
                (d_hbm, d_ref),
                (s_hbm, s_ref),
            )
        )
    ]

    recv_buf[...] = jnp.zeros(recv_buf.shape, F32)

    barrier = pltpu.get_barrier_semaphore()
    arrivals = jnp.int32(nz - 1)
    for offset, _, _, _ in MESSAGES:
        if offset[:2] == (0, 0):
            continue
        ok = exists(offset)
        arrivals = arrivals + ok.astype(jnp.int32)

        @pl.when(ok)
        def _(offset=offset):
            pl.semaphore_signal(barrier, inc=1, device_id=device(offset), device_id_type=MESH)

    for step in range(1, nz):
        pl.semaphore_signal(
            barrier, inc=1, device_id=(me[0], me[1], peer(step)), device_id_type=MESH
        )

    for load in loads:
        load.start()

    row = iota((8, 128), 0)
    lane = iota((8, 128), 1)
    planes = range(8)

    for load in loads[1:7]:
        load.wait()
    mat = [mat_ref[i] for i in planes]
    keep = [jnp.zeros((8, 128), F32) for _ in planes]
    gain = [jnp.zeros((8, 128), F32) for _ in planes]
    for m in range(eps_ref.shape[0]):
        loss = jnp.full((8, 128), loss_ref[m], F32)
        eps = jnp.full((8, 128), eps_ref[m], F32)
        keep_m = (1.0 - loss) / (1.0 + loss)
        gain_m = 0.5 / (eps * (1.0 + loss))
        for i in planes:
            same = mat[i] == m
            keep[i] = jnp.where(same, keep_m, keep[i])
            gain[i] = jnp.where(same, gain_m, gain[i])
    for i in planes:
        keep_ref[i] = keep[i]
        gain_ref[i] = gain[i]

    def pack_y(c, j):
        tile = jnp.zeros((8, 128), F32)
        for i in planes:
            tile = jnp.where(row == i, full(e_ref[c, i, j : j + 1, :]), tile)
        return tile

    def pack_z(comps, k):
        tile = jnp.zeros((8, 128), F32)
        for c in comps:
            for i in planes:
                tile = jnp.where(lane == c * 8 + i, full(e_ref[c, i][:, k : k + 1]), tile)
        return tile

    def pack_far(n):
        e_x7, e_z0 = e_ref[0, 7], e_ref[2, 0]
        tiles = {
            0: pltpu.roll(e_x7, 127, 1),
            2: pltpu.roll(e_z0, 24, 1),
            4: e_x7,
            5: e_ref[1, 7],
            6: e_ref[2, 7],
            8: e_ref[1, 0],
            9: e_z0,
            11: pltpu.roll(e_x7, 7, 0),
            13: e_ref[1, 0],
        }
        for t, tile in tiles.items():
            send_buf[n, t] = tile

    def pack_gains():
        send_buf[0, 1] = pltpu.roll(gain[7], 127, 1)
        send_buf[0, 3] = pltpu.roll(gain[0], 24, 1)
        send_buf[0, 7] = gain[7]
        send_buf[0, 10] = gain[0]
        send_buf[0, 12] = pltpu.roll(gain[7], 7, 0)

    def pack_near(n):
        y7 = [pack_y(c, 7) for c in range(3)]
        z127 = pack_z((0, 1, 2), 127)
        tiles = [pltpu.roll(z127, 7, 0), pltpu.roll(y7[1], 127, 1), z127, pack_z((0, 1), 0)]
        tiles += y7 + [pack_y(0, 0), pack_y(2, 0)]
        for t, tile in enumerate(tiles):
            send_buf[n, 14 + t] = tile

    def message(m, n):
        offset, first, count, more = MESSAGES[m]
        tiles = pl.ds(first, count + (more if n == 0 else 0))
        return pltpu.make_async_remote_copy(
            src_ref=send_buf.at[n, tiles],
            dst_ref=recv_buf.at[n, tiles],
            send_sem=send_sem.at[n, m],
            recv_sem=recv_sem.at[n, m],
            device_id=device(offset),
            device_id_type=MESH,
        )

    def send(which, n):
        for m in which:

            @pl.when(exists(MESSAGES[m][0]))
            def _(m=m):
                message(m, n).start()

    def wait_recv(which, n):
        for m in which:

            @pl.when(exists(tuple(-o for o in MESSAGES[m][0])))
            def _(m=m):
                message(m, n).wait_recv()

    def wait_send(n):
        for m in range(len(MESSAGES)):

            @pl.when(exists(MESSAGES[m][0]))
            def _(m=m):
                message(m, n).wait_send()

    loads[0].wait()
    pack_far(0)
    pack_gains()
    pack_near(0)

    ports = cell_ref.shape[0]
    owners = [owner_ref[q] for q in range(ports)]
    srow = iota((slots, 128), 0)
    slane = iota((slots, 128), 1)
    slot_cell = jnp.full((slots, 128), -1, jnp.int32)
    lane_cell = jnp.full((8, 128), -1, jnp.int32)
    for q in range(ports):
        index = owners[q] * cap
        for r in range(q):
            index = index + jnp.where(owners[r] == owners[q], 1, 0)
        slot_cell = jnp.where(srow == index, cell_ref[q], slot_cell)
        lane_cell = jnp.where(lax.rem(lane, slots) == index, cell_ref[q], lane_cell)
    in_lane = jnp.logical_and(slot_cell >= 0, (slot_cell & 127) == slane)
    gather = jnp.where((slot_cell >> 7) == lax.rem(slane, 64), 1.0, 0.0).astype(BF16)
    in_row = jnp.broadcast_to((lane_cell >> 7)[0:1, :], (64, 128))
    scatter = jnp.where(in_row == iota((64, 128), 0), 1.0, 0.0).astype(BF16)

    for load in loads[7:]:
        load.wait()
    brow = iota((slots + 8, 128), 0)
    which = jnp.where(brow == slots + 1, 1, 0)
    for s in range(slots):
        which = jnp.where(brow == s, block_ref[s], which)
    first = jnp.concatenate([which, which], axis=1) == 0
    nodes = x_ref.shape[1]
    state = jnp.concatenate(
        [x_ref[...], d_ref[...], jnp.zeros((6, nodes), F32)], axis=0
    )
    sense = jnp.where(
        first,
        jnp.broadcast_to(s_ref[0:1, :], first.shape),
        jnp.broadcast_to(s_ref[1:2, :], first.shape),
    )
    halves = [split(u_ref[b], 2) for b in range(2)]
    drives = [state[slots : slots + 2]]
    readouts = [jnp.sum(state * sense, axis=1, keepdims=True)]
    for n in range(ITERS):
        hi, lo = split(state, 2)
        both = [
            dot_t(hi, high) + (dot_t(hi, low) + dot_t(lo, high)) for high, low in halves
        ]
        state = jnp.where(first, both[0], both[1])
        readouts.append(jnp.sum(state * sense, axis=1, keepdims=True))
        if n < ITERS - 1:
            drives.append(state[slots : slots + 2])
    base_ref[...] = state[:slots]
    is_first = first[:slots, :128]
    coefs = jnp.zeros((slots, 128), F32)
    for n in range(ITERS):
        coefs = jnp.where(slane == n, readouts[n + 1][:slots], coefs)
        kick = jnp.where(is_first, readouts[n][slots : slots + 1], readouts[n][slots + 1 : slots + 2])
        coefs = jnp.where(slane == ITERS + n, kick, coefs)
    for g in range(nz):
        coef_send[g] = coefs[g * cap : (g + 1) * cap]

    pl.semaphore_wait(barrier, arrivals)

    send(FAR, 0)
    send(NEAR, 0)

    def exchange(step, src, dst, ssem, rsem):
        there = peer(step)
        return pltpu.make_async_remote_copy(
            src_ref=src.at[there],
            dst_ref=dst.at[me[2]],
            send_sem=ssem.at[step],
            recv_sem=rsem.at[step],
            device_id=(me[0], me[1], there),
            device_id_type=MESH,
        )

    coef_copies = [
        exchange(step, coef_send, coef_recv, coef_ssem, coef_rsem) for step in range(1, nz)
    ]
    for copy in coef_copies:
        copy.start()
    coef_recv[me[2]] = coef_send[me[2]]

    low = [jnp.where(me[d] > 0, 1.0, 0.0).astype(F32) for d in range(3)]
    ghosts = None
    owed = None
    volts = []

    def lacking(where, tile, value):
        return jnp.where(where, 0.5 * recv_buf[0, tile], 0.0) * value

    for n in range(ITERS):
        e_z = [e_ref[2, i] for i in planes]
        for i in planes:
            hist_ref[n, i] = e_z[i]
        stack = jnp.concatenate(e_z, axis=0)
        found = dot(gather, jnp.concatenate(split(stack, 2), axis=0))
        volts.append(
            jnp.sum(jnp.where(in_lane, found, 0.0), axis=1, keepdims=True)
        )
        if n == ITERS - 1:
            tile = jnp.zeros((slots, 128), F32)
            for k in range(ITERS):
                tile = jnp.where(slane == k, volts[k], tile)
            for g in range(nz):
                volt_send[g] = tile[g * cap : (g + 1) * cap]
            volt_copies = [
                exchange(step, volt_send, volt_recv, volt_ssem, volt_rsem)
                for step in range(1, nz)
            ]
            for copy in volt_copies:
                copy.start()
            volt_recv[me[2]] = volt_send[me[2]]

        wait_recv([m for m in range(len(MESSAGES)) if m not in LATE], n)

        def got(t, n=n):
            return recv_buf[n, t]

        ex_m, ey_m, ez_m = got(4), got(5), got(6)
        ey_p, ez_p = got(8), got(9)
        ex_edge = got(11)
        if n > 0:
            ex_m, ez_p, ex_edge = ex_m + owed[0], ez_p + owed[1], ex_edge + owed[2]
        ex_k = jnp.where(lane == 127, 0.0, pltpu.roll(ex_m, 127, 1))
        ex_j = jnp.where(row == 7, ex_edge, pltpu.roll(ex_m, 7, 0))
        hy_x = -0.5 * ((ex_k - ex_m) - (e_ref[2, 0] - ez_m))
        hz_x = -0.5 * ((e_ref[1, 0] - ey_m) - (ex_j - ex_m))
        fx_m, fy_m, fz_m = got(18), got(19), got(20)
        fx_0, fz_0 = send_buf[n, 21], send_buf[n, 22]
        fy_k = jnp.where(lane == 127, got(15), pltpu.roll(fy_m, 127, 1))
        fy_i = jnp.where(row == 7, got(13), pltpu.roll(fy_m, 7, 0))
        hx_y = -0.5 * ((fz_0 - fz_m) - (fy_k - fy_m))
        hz_y = -0.5 * ((fy_i - fy_m) - (fx_0 - fx_m))
        g_m, g_0, g_edge = got(16), send_buf[n, 17], got(14)
        gz_j = jnp.where(row == 7, g_edge, pltpu.roll(g_m, 7, 0)) - g_m
        gz_i = jnp.where(lane == 23, 0.0, pltpu.roll(g_m, 127, 1)) - g_m
        g_d = g_0 - g_m
        h_z = -0.5 * jnp.where(
            lane < 8, g_d - pltpu.roll(gz_i, 128 - 16, 1), pltpu.roll(gz_j, 128 - 8, 1) - g_d
        )
        new = [hy_x * low[0], hz_x * low[0], hx_y * low[1], hz_y * low[1], h_z * low[2]]
        ghosts = new if ghosts is None else [a + b for a, b in zip(ghosts, new)]
        hy_x, hz_x, hx_y, hz_y, h_z = ghosts

        zp = got(17)
        was_owed = owed
        if n < ITERS - 1:
            owed = [
                lacking(lane == 0, 7, pltpu.roll(g_m, 112, 1)),
                lacking(lane == 127, 10, pltpu.roll(zp, 120, 1)),
                lacking(jnp.logical_and(lane == 0, row == 7), 12, pltpu.roll(g_edge, 112, 1)),
                e_ref[2, 0],
                pltpu.roll(e_ref[0, 7], 23, 1),
            ]

        for i in planes:
            ex, ey, ez = e_ref[0, i], e_ref[1, i], e_ref[2, i]
            ex_j = jnp.where(row == 7, full(recv_buf[n, 21, i : i + 1, :]), pltpu.roll(ex, 7, 0))
            ez_j = jnp.where(row == 7, full(recv_buf[n, 22, i : i + 1, :]), pltpu.roll(ez, 7, 0))
            ex_k = jnp.where(lane == 127, full(zp[:, i : i + 1]), pltpu.roll(ex, 127, 1))
            ey_k = jnp.where(lane == 127, full(zp[:, 8 + i : 9 + i]), pltpu.roll(ey, 127, 1))
            ey_i = e_ref[1, i + 1] if i < 7 else ey_p
            ez_i = e_ref[2, i + 1] if i < 7 else ez_p
            hx = -0.5 * ((ez_j - ez) - (ey_k - ey))
            hy = -0.5 * ((ex_k - ex) - (ez_i - ez))
            hz = -0.5 * ((ey_i - ey) - (ex_j - ex))
            for c, value in enumerate((hx, hy, hz)):
                h_ref[c, i] = value if n == 0 else h_ref[c, i] + value

        if n == 0:
            for copy in coef_copies:
                copy.wait_recv()
            for g in range(nz):
                gather_buf[g * cap : (g + 1) * cap, :] = coef_recv[g]
            table = gather_buf[...]
            spread = jnp.concatenate(
                [
                    jnp.where(in_lane, jnp.broadcast_to(table[:, k : k + 1], (slots, 128)), 0.0)
                    for k in range(2 * ITERS)
                ],
                axis=1,
            )
            pieces = split(spread, 3) + [jnp.zeros(spread.shape, BF16)]
            field_ref[...] = dot(scatter, jnp.concatenate(pieces, axis=0))

        for i in planes:
            hx, hy, hz = h_ref[0, i], h_ref[1, i], h_ref[2, i]
            hx_j = jnp.where(row == 0, full(hx_y[i : i + 1, :]), pltpu.roll(hx, 1, 0))
            hz_j = jnp.where(row == 0, full(hz_y[i : i + 1, :]), pltpu.roll(hz, 1, 0))
            hy_k = jnp.where(lane == 0, full(h_z[:, i : i + 1]), pltpu.roll(hy, 1, 1))
            hx_k = jnp.where(lane == 0, full(h_z[:, 8 + i : 9 + i]), pltpu.roll(hx, 1, 1))
            hy_i = h_ref[1, i - 1] if i > 0 else hy_x
            hz_i = h_ref[2, i - 1] if i > 0 else hz_x
            rows = slice(8 * i, 8 * i + 8)
            current = field_ref[rows, 128 * n : 128 * (n + 1)]
            for k in range(n + 1):
                at = ITERS + n - k
                current = current + field_ref[rows, 128 * at : 128 * (at + 1)] * hist_ref[k, i]
            keep, gain = keep_ref[i], gain_ref[i]
            e_ref[0, i] = keep * e_ref[0, i] + gain * ((hz - hz_j) - (hy - hy_k))
            e_ref[1, i] = keep * e_ref[1, i] + gain * ((hx - hx_k) - (hz - hz_i))
            e_ref[2, i] = keep * e_ref[2, i] + gain * (((hy - hy_i) - (hx - hx_j)) - current)

        if n < ITERS - 1:
            pack_far(n + 1)
            send(FAR, n + 1)

        wait_recv(LATE, n)
        x_edge, z_edge = got(0), got(2)
        if n > 0:
            x_edge = x_edge + lacking(lane == 127, 1, was_owed[3])
            z_edge = z_edge + lacking(lane == 23, 3, was_owed[4])
        x_edge = jnp.where(lane == 127, 0.5 * low[0] * x_edge, 0.0)
        z_edge = jnp.where(lane == 23, 0.5 * low[2] * z_edge, 0.0)
        ghosts[0] = ghosts[0] - x_edge
        ghosts[4] = ghosts[4] + pltpu.roll(z_edge, 112, 1)
        e_ref[2, 0] = e_ref[2, 0] + gain_ref[0] * x_edge
        e_ref[0, 7] = e_ref[0, 7] + gain_ref[7] * pltpu.roll(z_edge, 105, 1)

        if n < ITERS - 1:
            pack_near(n + 1)
            send(NEAR, n + 1)

    for copy in volt_copies:
        copy.wait_recv()
    for g in range(nz):
        gather_buf[g * cap : (g + 1) * cap, :] = volt_recv[g]
    table = gather_buf[...]
    final = base_ref[...]
    pick = first[:slots]
    for k in range(ITERS):
        drive = drives[ITERS - 1 - k]
        rows = jnp.where(
            pick,
            jnp.broadcast_to(drive[0:1], final.shape),
            jnp.broadcast_to(drive[1:2], final.shape),
        )
        final = final + rows * table[:, k : k + 1]
    base_ref[...] = final
    for copy in coef_copies + volt_copies:
        copy.wait_send()
    for n in range(ITERS):
        wait_send(n)


def hand_out(*refs):
    sources, results, sem = refs[:3], refs[3:6], refs[6]
    copies = [
        pltpu.make_async_copy(src, dst, sem.at[n])
        for n, (src, dst) in enumerate(zip(sources, results))
    ]
    for copy in copies:
        copy.start()
    for copy in copies:
        copy.wait()


def solution(mesh):
    sizes = tuple(mesh.shape[a] for a in AXES)

    def local(
        e_field,
        material,
        permittivity,
        loss,
        port_cell,
        port_owner,
        circuit_block,
        circuit_state,
        mna_update,
        mna_drive,
        mna_sense,
    ):
        slots, nodes = circuit_state.shape
        cap = slots // sizes[2]
        hbm = pl.BlockSpec(memory_space=pltpu.HBM)
        dma = pltpu.SemaphoreType.DMA
        vmem = pl.BlockSpec(memory_space=pltpu.VMEM)
        shapes = (e_field.shape, e_field.shape, circuit_state.shape)
        results = pl.pallas_call(
            functools.partial(kernel, sizes),
            out_shape=[pltpu.VMEM(shape, F32) for shape in shapes],
            in_specs=[hbm] * 11,
            out_specs=[vmem] * 3,
            scratch_shapes=[
                pltpu.SMEM(permittivity.shape, F32),
                pltpu.SMEM(loss.shape, F32),
                pltpu.SMEM(port_cell.shape, jnp.int32),
                pltpu.SMEM(port_cell.shape, jnp.int32),
                pltpu.SMEM(circuit_block.shape, jnp.int32),
                pltpu.VMEM(material.shape, jnp.int32),
                pltpu.VMEM(material.shape, F32),
                pltpu.VMEM(material.shape, F32),
                pltpu.VMEM((ITERS,) + material.shape, F32),
                pltpu.VMEM((64, 2 * ITERS * 128), F32),
                pltpu.VMEM(circuit_state.shape, F32),
                pltpu.VMEM(mna_update.shape, F32),
                pltpu.VMEM(mna_drive.shape, F32),
                pltpu.VMEM(mna_sense.shape, F32),
                pltpu.VMEM((ITERS, TILES, 8, 128), F32),
                pltpu.VMEM((ITERS, TILES, 8, 128), F32),
                pltpu.VMEM((sizes[2], cap, 128), F32),
                pltpu.VMEM((sizes[2], cap, 128), F32),
                pltpu.VMEM((sizes[2], cap, 128), F32),
                pltpu.VMEM((sizes[2], cap, 128), F32),
                pltpu.VMEM((slots, 128), F32),
                dma((11,)),
                dma((ITERS, len(MESSAGES))),
                dma((ITERS, len(MESSAGES))),
                dma((sizes[2],)),
                dma((sizes[2],)),
                dma((sizes[2],)),
                dma((sizes[2],)),
            ],
            compiler_params=pltpu.CompilerParams(
                collective_id=0, has_side_effects=True, vmem_limit_bytes=32 * 1024 * 1024
            ),
        )(
            *(
                pltpu.with_memory_space_constraint(array, pltpu.HBM)
                for array in (
                    e_field,
                    material,
                    permittivity,
                    loss,
                    port_cell,
                    port_owner.reshape(-1),
                    circuit_block,
                    circuit_state,
                    mna_update,
                    mna_drive,
                    mna_sense,
                )
            )
        )
        return pl.pallas_call(
            hand_out,
            out_shape=[jax.ShapeDtypeStruct(shape, F32) for shape in shapes],
            in_specs=[vmem] * 3,
            out_specs=[hbm] * 3,
            scratch_shapes=[dma((3,))],
        )(*(pltpu.with_memory_space_constraint(r, pltpu.VMEM) for r in results))

    placed = (
        P(None, "gx", "gy", "gz"),
        P("gx", "gy", "gz"),
        P(),
        P(),
        P(("gx", "gy", "gz")),
        P(("gx", "gy", "gz"), None),
        P(("gx", "gy", "gz")),
        P(("gx", "gy", "gz"), None),
        P(("gx", "gy", "gz"), None, None),
        P(("gx", "gy", "gz"), None),
        P(("gx", "gy", "gz"), None),
    )
    return jax.shard_map(
        local,
        mesh=mesh,
        in_specs=placed,
        out_specs=(
            P(None, "gx", "gy", "gz"),
            P(None, "gx", "gy", "gz"),
            P(("gx", "gy", "gz"), None),
        ),
        check_vma=False,
    )
```

```python
import functools

import jax
import jax.numpy as jnp
from jax import lax
from jax.experimental import pallas as pl
from jax.experimental.pallas import tpu as pltpu
from jax.sharding import PartitionSpec as P

ITERS = 4
MESH = pl.DeviceIdType.MESH
AXES = ("gx", "gy", "gz")
F32 = jnp.float32
BF16 = jnp.bfloat16

MESSAGES = (
    ((1, 0, -1), 0, 1, 1),
    ((-1, 0, 1), 2, 1, 1),
    ((1, 0, 0), 4, 3, 1),
    ((-1, 0, 0), 8, 2, 1),
    ((1, -1, 0), 11, 1, 1),
    ((-1, 1, 0), 13, 1, 0),
    ((0, -1, 1), 14, 1, 0),
    ((0, 1, -1), 15, 1, 0),
    ((0, 0, 1), 16, 1, 0),
    ((0, 0, -1), 17, 1, 0),
    ((0, 1, 0), 18, 3, 0),
    ((0, -1, 0), 21, 2, 0),
)
TILES = 23
LATE = (0, 1)
FAR = range(6)
NEAR = range(6, 12)

def iota(shape, dim):
    return lax.broadcasted_iota(jnp.int32, shape, dim)


def full(row):
    return jnp.broadcast_to(row, (8, 128))


def split(value, parts):
    pieces = []
    for _ in range(parts):
        piece = value.astype(BF16)
        pieces.append(piece)
        value = value - piece.astype(F32)
    return pieces


def dot(a, b):
    return jnp.dot(a, b, preferred_element_type=F32)


def dot_t(a, b):
    return lax.dot_general(a, b, (((1,), (1,)), ((), ())), preferred_element_type=F32)


def kernel(
    sizes,
    e_hbm,
    mat_hbm,
    eps_hbm,
    loss_hbm,
    cell_hbm,
    owner_hbm,
    block_hbm,
    x_hbm,
    u_hbm,
    d_hbm,
    s_hbm,
    e_ref,
    h_ref,
    base_ref,
    eps_ref,
    loss_ref,
    cell_ref,
    owner_ref,
    block_ref,
    mat_ref,
    keep_ref,
    gain_ref,
    hist_ref,
    field_ref,
    x_ref,
    u_ref,
    d_ref,
    s_ref,
    send_buf,
    recv_buf,
    coef_send,
    coef_recv,
    volt_send,
    volt_recv,
    gather_buf,
    in_sem,
    send_sem,
    recv_sem,
    coef_ssem,
    coef_rsem,
    volt_ssem,
    volt_rsem,
    peers_sem,
    faces_sem,
):
    nz = sizes[2]
    cap = x_ref.shape[0] // nz
    slots = x_ref.shape[0]
    me = [lax.axis_index(a) for a in AXES]

    def exists(offset, place=me):
        ok = None
        for at, off, size in zip(place, offset, sizes):
            if off:
                one = at + off >= 0 if off < 0 else at + off < size
                ok = one if ok is None else jnp.logical_and(ok, one)
        return ok

    def device(offset):
        return tuple(at + off for at, off in zip(me, offset))

    def peer(step):
        return lax.rem(me[2] + step, nz)

    others = sorted(range(1, nz), key=lambda step: -min(step, nz - step))

    loads = [
        pltpu.make_async_copy(src, dst, in_sem.at[n])
        for n, (src, dst) in enumerate(
            (
                (e_hbm, e_ref),
                (mat_hbm, mat_ref),
                (eps_hbm, eps_ref),
                (loss_hbm, loss_ref),
                (cell_hbm, cell_ref),
                (owner_hbm, owner_ref),
                (block_hbm, block_ref),
                (u_hbm, u_ref),
                (x_hbm, x_ref),
                (d_hbm, d_ref),
                (s_hbm, s_ref),
            )
        )
    ]

    recv_buf[...] = jnp.zeros(recv_buf.shape, F32)

    barrier = pltpu.get_barrier_semaphore()
    odd = lax.rem(me[1], 2)
    is_even, is_odd = odd == 0, odd == 1
    sibling = (me[0], me[1] + 1 - 2 * odd, me[2])
    neighbours = jnp.int32(-1)
    for offset, _, _, _ in MESSAGES:
        ok = exists(offset)
        neighbours = neighbours + ok.astype(jnp.int32)
        neighbours = neighbours + exists(offset, (me[0], me[1] + 1, me[2])).astype(jnp.int32)
        if offset == (0, 1, 0):
            ok = jnp.logical_and(ok, is_odd)

        @pl.when(ok)
        def _(offset=offset):
            there = device(offset)
            pl.semaphore_signal(
                barrier,
                inc=1,
                device_id=(there[0], there[1] - lax.rem(there[1], 2), there[2]),
                device_id_type=MESH,
            )

    for step in others:
        pl.semaphore_signal(
            barrier, inc=1, device_id=(me[0], me[1] + 1 - odd, peer(step)), device_id_type=MESH
        )

    @pl.when(is_even)
    def _():
        pl.semaphore_signal(barrier, inc=1, device_id=sibling, device_id_type=MESH)

    for load in loads:
        load.start()

    row = iota((8, 128), 0)
    lane = iota((8, 128), 1)
    planes = range(8)

    for load in loads[1:7]:
        load.wait()
    mat = [mat_ref[i] for i in planes]
    keep = [jnp.zeros((8, 128), F32) for _ in planes]
    gain = [jnp.zeros((8, 128), F32) for _ in planes]
    for m in range(eps_ref.shape[0]):
        loss = jnp.full((8, 128), loss_ref[m], F32)
        eps = jnp.full((8, 128), eps_ref[m], F32)
        keep_m = (1.0 - loss) / (1.0 + loss)
        gain_m = 0.5 / (eps * (1.0 + loss))
        for i in planes:
            same = mat[i] == m
            keep[i] = jnp.where(same, keep_m, keep[i])
            gain[i] = jnp.where(same, gain_m, gain[i])
    for i in planes:
        keep_ref[i] = keep[i]
        gain_ref[i] = gain[i]

    def pack_y(c, j):
        tile = jnp.zeros((8, 128), F32)
        for i in planes:
            tile = jnp.where(row == i, full(e_ref[c, i, j : j + 1, :]), tile)
        return tile

    def pack_z(comps, k):
        tile = jnp.zeros((8, 128), F32)
        for c in comps:
            for i in planes:
                tile = jnp.where(lane == c * 8 + i, full(e_ref[c, i][:, k : k + 1]), tile)
        return tile

    def pack_far(n):
        e_x7, e_z0 = e_ref[0, 7], e_ref[2, 0]
        tiles = {
            0: pltpu.roll(e_x7, 127, 1),
            2: pltpu.roll(e_z0, 24, 1),
            4: e_x7,
            5: e_ref[1, 7],
            6: e_ref[2, 7],
            8: e_ref[1, 0],
            9: e_z0,
            11: pltpu.roll(e_x7, 7, 0),
            13: e_ref[1, 0],
        }
        for t, tile in tiles.items():
            send_buf[n, t] = tile

    def pack_gains():
        send_buf[0, 1] = pltpu.roll(gain[7], 127, 1)
        send_buf[0, 3] = pltpu.roll(gain[0], 24, 1)
        send_buf[0, 7] = gain[7]
        send_buf[0, 10] = gain[0]
        send_buf[0, 12] = pltpu.roll(gain[7], 7, 0)

    def pack_near(n):
        y7 = [pack_y(c, 7) for c in range(3)]
        z127 = pack_z((0, 1, 2), 127)
        tiles = [pltpu.roll(z127, 7, 0), pltpu.roll(y7[1], 127, 1), z127, pack_z((0, 1), 0)]
        tiles += y7 + [pack_y(0, 0), pack_y(2, 0)]
        for t, tile in enumerate(tiles):
            send_buf[n, 14 + t] = tile

    def message(m, n):
        offset, first, count, more = MESSAGES[m]
        tiles = pl.ds(first, count + (more if n == 0 else 0))
        return pltpu.make_async_remote_copy(
            src_ref=send_buf.at[n, tiles],
            dst_ref=recv_buf.at[n, tiles],
            send_sem=send_sem.at[n, m],
            recv_sem=recv_sem.at[n, m],
            device_id=device(offset),
            device_id_type=MESH,
        )

    def send(which, n):
        for m in which:

            @pl.when(exists(MESSAGES[m][0]))
            def _(m=m):
                message(m, n).start()

    def wait_recv(which, n):
        for m in which:

            @pl.when(exists(tuple(-o for o in MESSAGES[m][0])))
            def _(m=m):
                message(m, n).wait_recv()

    def wait_send(n):
        for m in range(len(MESSAGES)):

            @pl.when(exists(MESSAGES[m][0]))
            def _(m=m):
                message(m, n).wait_send()

    loads[0].wait()
    pack_far(0)
    pack_gains()
    pack_near(0)

    ports = cell_ref.shape[0]
    owners = [owner_ref[q] for q in range(ports)]
    srow = iota((slots, 128), 0)
    slane = iota((slots, 128), 1)
    slot_cell = jnp.full((slots, 128), -1, jnp.int32)
    lane_cell = jnp.full((8, 128), -1, jnp.int32)
    for q in range(ports):
        index = owners[q] * cap
        for r in range(q):
            index = index + jnp.where(owners[r] == owners[q], 1, 0)
        slot_cell = jnp.where(srow == index, cell_ref[q], slot_cell)
        lane_cell = jnp.where(lax.rem(lane, slots) == index, cell_ref[q], lane_cell)
    in_lane = jnp.logical_and(slot_cell >= 0, (slot_cell & 127) == slane)
    gather = jnp.where((slot_cell >> 7) == lax.rem(slane, 64), 1.0, 0.0).astype(BF16)
    in_row = jnp.broadcast_to((lane_cell >> 7)[0:1, :], (64, 128))
    scatter = jnp.where(in_row == iota((64, 128), 0), 1.0, 0.0).astype(BF16)

    for load in loads[7:]:
        load.wait()
    brow = iota((slots + 8, 128), 0)
    which = jnp.where(brow == slots + 1, 1, 0)
    for s in range(slots):
        which = jnp.where(brow == s, block_ref[s], which)
    first = jnp.concatenate([which, which], axis=1) == 0
    nodes = x_ref.shape[1]
    state = jnp.concatenate(
        [x_ref[...], d_ref[...], jnp.zeros((6, nodes), F32)], axis=0
    )
    sense = jnp.where(
        first,
        jnp.broadcast_to(s_ref[0:1, :], first.shape),
        jnp.broadcast_to(s_ref[1:2, :], first.shape),
    )
    halves = [split(u_ref[b], 2) for b in range(2)]
    drives = [state[slots : slots + 2]]
    readouts = [jnp.sum(state * sense, axis=1, keepdims=True)]
    for n in range(ITERS):
        hi, lo = split(state, 2)
        both = [
            dot_t(hi, high) + (dot_t(hi, low) + dot_t(lo, high)) for high, low in halves
        ]
        state = jnp.where(first, both[0], both[1])
        readouts.append(jnp.sum(state * sense, axis=1, keepdims=True))
        if n < ITERS - 1:
            drives.append(state[slots : slots + 2])
    base_ref[...] = state[:slots]
    is_first = first[:slots, :128]
    coefs = jnp.zeros((slots, 128), F32)
    for n in range(ITERS):
        coefs = jnp.where(slane == n, readouts[n + 1][:slots], coefs)
        kick = jnp.where(is_first, readouts[n][slots : slots + 1], readouts[n][slots + 1 : slots + 2])
        coefs = jnp.where(slane == ITERS + n, kick, coefs)
    for g in range(nz):
        coef_send[g] = coefs[g * cap : (g + 1) * cap]

    def exchange(step, src, dst, ssem, rsem):
        there = peer(step)
        return pltpu.make_async_remote_copy(
            src_ref=src.at[there],
            dst_ref=dst.at[me[2]],
            send_sem=ssem.at[step],
            recv_sem=rsem.at[step],
            device_id=(me[0], me[1], there),
            device_id_type=MESH,
        )

    coef_copies = [
        exchange(step, coef_send, coef_recv, coef_ssem, coef_rsem) for step in others
    ]
    coef_recv[me[2]] = coef_send[me[2]]

    def start_circuits():
        @pl.when(is_odd)
        def _():
            pl.semaphore_wait(barrier, 2 * (nz - 1) + 1)
            pl.semaphore_signal(peers_sem, inc=1, device_id=sibling, device_id_type=MESH)

        @pl.when(is_even)
        def _():
            pl.semaphore_wait(peers_sem, 1)

        for copy in coef_copies:
            copy.start()

    def start_faces():
        @pl.when(is_even)
        def _():
            pl.semaphore_wait(barrier, neighbours)
            pl.semaphore_signal(faces_sem, inc=1, device_id=sibling, device_id_type=MESH)

        @pl.when(is_odd)
        def _():
            pl.semaphore_wait(faces_sem, 1)

        send(FAR, 0)
        send(NEAR, 0)

    last = me[2] >= nz - 2
    pl.when(last)(start_circuits)
    start_faces()
    pl.when(jnp.logical_not(last))(start_circuits)

    low = [jnp.where(me[d] > 0, 1.0, 0.0).astype(F32) for d in range(3)]
    ghosts = None
    owed = None
    volts = []

    def lacking(where, tile, value):
        return jnp.where(where, 0.5 * recv_buf[0, tile], 0.0) * value

    def voltages(n):
        e_z = [e_ref[2, i] for i in planes]
        for i in planes:
            hist_ref[n, i] = e_z[i]
        stack = jnp.concatenate(e_z, axis=0)
        found = dot(gather, jnp.concatenate(split(stack, 2), axis=0))
        volts.append(jnp.sum(jnp.where(in_lane, found, 0.0), axis=1, keepdims=True))

    def send_voltages():
        tile = jnp.zeros((slots, 128), F32)
        for k in range(ITERS):
            tile = jnp.where(slane == k, volts[k], tile)
        for g in range(nz):
            volt_send[g] = tile[g * cap : (g + 1) * cap]
        copies = [exchange(step, volt_send, volt_recv, volt_ssem, volt_rsem) for step in others]
        for copy in copies:
            copy.start()
        volt_recv[me[2]] = volt_send[me[2]]
        return copies

    def fields(table, ks):
        spread = jnp.concatenate(
            [
                jnp.where(in_lane, jnp.broadcast_to(table[:, k : k + 1], (slots, 128)), 0.0)
                for k in ks
            ],
            axis=1,
        )
        pieces = split(spread, 3) + [jnp.zeros(spread.shape, BF16)]
        found = dot(scatter, jnp.concatenate(pieces, axis=0))
        for at, k in enumerate(ks):
            field_ref[:, 128 * k : 128 * (k + 1)] = found[:, 128 * at : 128 * (at + 1)]

    voltages(0)
    for n in range(ITERS):
        if n == ITERS - 1 and n == 0:
            volt_copies = send_voltages()

        def got(t, n=n):
            return recv_buf[n, t]

        wait_recv(NEAR, n)

        fx_m, fy_m, fz_m = got(18), got(19), got(20)
        fx_0, fz_0 = send_buf[n, 21], send_buf[n, 22]
        fy_k = jnp.where(lane == 127, got(15), pltpu.roll(fy_m, 127, 1))
        hx_y = -0.5 * ((fz_0 - fz_m) - (fy_k - fy_m)) * low[1]
        fy_i = jnp.where(row == 7, 0.0, pltpu.roll(fy_m, 7, 0))
        hz_y = -0.5 * ((fy_i - fy_m) - (fx_0 - fx_m)) * low[1]
        g_m, g_0, g_edge = got(16), send_buf[n, 17], got(14)
        gz_j = jnp.where(row == 7, g_edge, pltpu.roll(g_m, 7, 0)) - g_m
        gz_i = jnp.where(lane == 23, 0.0, pltpu.roll(g_m, 127, 1)) - g_m
        g_d = g_0 - g_m
        h_z = -0.5 * low[2] * jnp.where(
            lane < 8, g_d - pltpu.roll(gz_i, 128 - 16, 1), pltpu.roll(gz_j, 128 - 8, 1) - g_d
        )
        if n > 0:
            hx_y, hz_y, h_z = hx_y + ghosts[2], hz_y + ghosts[3], h_z + ghosts[4]

        zp = got(17)
        was_owed = owed
        owed = [None] * 5
        if n < ITERS - 1:
            owed[3:] = [e_ref[2, 0], pltpu.roll(e_ref[0, 7], 23, 1)]

        def update_h(i, ey_i, ez_i, which, n=n, zp=zp):
            ex, ey, ez = e_ref[0, i], e_ref[1, i], e_ref[2, i]
            if 0 in which:
                ez_j = jnp.where(
                    row == 7, full(recv_buf[n, 22, i : i + 1, :]), pltpu.roll(ez, 7, 0)
                )
                ey_k = jnp.where(lane == 127, full(zp[:, 8 + i : 9 + i]), pltpu.roll(ey, 127, 1))
                hx = -0.5 * ((ez_j - ez) - (ey_k - ey))
                h_ref[0, i] = hx if n == 0 else h_ref[0, i] + hx
            if 1 in which:
                ex_j = jnp.where(
                    row == 7, full(recv_buf[n, 21, i : i + 1, :]), pltpu.roll(ex, 7, 0)
                )
                ex_k = jnp.where(lane == 127, full(zp[:, i : i + 1]), pltpu.roll(ex, 127, 1))
                hy = -0.5 * ((ex_k - ex) - (ez_i - ez))
                hz = -0.5 * ((ey_i - ey) - (ex_j - ex))
                h_ref[1, i] = hy if n == 0 else h_ref[1, i] + hy
                h_ref[2, i] = hz if n == 0 else h_ref[2, i] + hz

        def update_e(i, hy_i, hz_i, hx_y, hz_y, h_z, n=n):
            hx, hy, hz = h_ref[0, i], h_ref[1, i], h_ref[2, i]
            hx_j = jnp.where(row == 0, full(hx_y[i : i + 1, :]), pltpu.roll(hx, 1, 0))
            hz_j = jnp.where(row == 0, full(hz_y[i : i + 1, :]), pltpu.roll(hz, 1, 0))
            hy_k = jnp.where(lane == 0, full(h_z[:, i : i + 1]), pltpu.roll(hy, 1, 1))
            hx_k = jnp.where(lane == 0, full(h_z[:, 8 + i : 9 + i]), pltpu.roll(hx, 1, 1))
            rows = slice(8 * i, 8 * i + 8)
            current = field_ref[rows, 128 * n : 128 * (n + 1)]
            for k in range(n + 1):
                at = ITERS + n - k
                current = current + field_ref[rows, 128 * at : 128 * (at + 1)] * hist_ref[k, i]
            keep_i, gain_i = keep_ref[i], gain_ref[i]
            e_ref[0, i] = keep_i * e_ref[0, i] + gain_i * ((hz - hz_j) - (hy - hy_k))
            e_ref[1, i] = keep_i * e_ref[1, i] + gain_i * ((hx - hx_k) - (hz - hz_i))
            e_ref[2, i] = keep_i * e_ref[2, i] + gain_i * (((hy - hy_i) - (hx - hx_j)) - current)

        for i in range(7):
            update_h(i, e_ref[1, i + 1], e_ref[2, i + 1], (0, 1))
        update_h(7, None, None, (0,))
        if n == 0:
            for copy in coef_copies:
                copy.wait_recv()
            for g in range(nz):
                gather_buf[g * cap : (g + 1) * cap, :] = coef_recv[g]
            fields(gather_buf[...], [0, ITERS])
        e_0 = [e_ref[c, 0] for c in range(3)]
        for i in range(1, 7):
            update_e(i, h_ref[1, i - 1], h_ref[2, i - 1], hx_y, hz_y, h_z)

        wait_recv([m for m in FAR if m not in LATE], n)
        ex_m, ey_m, ez_m = got(4), got(5), got(6)
        ey_p, ez_p = got(8), got(9)
        ex_edge = got(11)
        if n > 0:
            ex_m, ez_p, ex_edge = ex_m + was_owed[0], ez_p + was_owed[1], ex_edge + was_owed[2]
        update_h(7, ey_p, ez_p, (1,))
        ex_k = jnp.where(lane == 127, 0.0, pltpu.roll(ex_m, 127, 1))
        ex_j = jnp.where(row == 7, ex_edge, pltpu.roll(ex_m, 7, 0))
        hy_x = -0.5 * ((ex_k - ex_m) - (e_0[2] - ez_m)) * low[0]
        hz_x = -0.5 * ((e_0[1] - ey_m) - (ex_j - ex_m)) * low[0]
        hz_y = hz_y - jnp.where(row == 7, 0.5 * low[1] * got(13), 0.0)
        if n > 0:
            hy_x, hz_x = hy_x + ghosts[0], hz_x + ghosts[1]
        ghosts = [hy_x, hz_x, hx_y, hz_y, h_z]
        update_e(0, hy_x, hz_x, hx_y, hz_y, h_z)
        update_e(7, h_ref[1, 6], h_ref[2, 6], hx_y, hz_y, h_z)

        if n < ITERS - 1:
            pack_far(n + 1)
            send(FAR, n + 1)
            owed[:3] = [
                lacking(lane == 0, 7, pltpu.roll(g_m, 112, 1)),
                lacking(lane == 127, 10, pltpu.roll(zp, 120, 1)),
                lacking(jnp.logical_and(lane == 0, row == 7), 12, pltpu.roll(g_edge, 112, 1)),
            ]
        if n == 0 and ITERS > 1:
            fields(gather_buf[...], [k for k in range(2 * ITERS) if k not in (0, ITERS)])

        wait_recv(LATE, n)
        x_edge, z_edge = got(0), got(2)
        if n > 0:
            x_edge = x_edge + lacking(lane == 127, 1, was_owed[3])
            z_edge = z_edge + lacking(lane == 23, 3, was_owed[4])
        x_edge = jnp.where(lane == 127, 0.5 * low[0] * x_edge, 0.0)
        z_edge = jnp.where(lane == 23, 0.5 * low[2] * z_edge, 0.0)
        ghosts[0] = ghosts[0] - x_edge
        ghosts[4] = ghosts[4] + pltpu.roll(z_edge, 112, 1)
        e_ref[2, 0] = e_ref[2, 0] + gain_ref[0] * x_edge
        e_ref[0, 7] = e_ref[0, 7] + gain_ref[7] * pltpu.roll(z_edge, 105, 1)

        if n < ITERS - 1:
            if n == ITERS - 2:
                voltages(n + 1)
                volt_copies = send_voltages()
            pack_near(n + 1)
            send(NEAR, n + 1)
            if n < ITERS - 2:
                voltages(n + 1)

    final = base_ref[...]
    pick = first[:slots]
    rows = [
        jnp.where(
            pick,
            jnp.broadcast_to(drive[0:1], final.shape),
            jnp.broadcast_to(drive[1:2], final.shape),
        )
        for drive in reversed(drives)
    ]
    for copy in volt_copies:
        copy.wait_recv()
    for g in range(nz):
        gather_buf[g * cap : (g + 1) * cap, :] = volt_recv[g]
    table = gather_buf[...]
    for k in range(ITERS):
        final = final + rows[k] * table[:, k : k + 1]
    base_ref[...] = final
    for copy in coef_copies + volt_copies:
        copy.wait_send()
    for n in range(ITERS):
        wait_send(n)


def hand_out(*refs):
    sources, results, sem = refs[:3], refs[3:6], refs[6]
    copies = [
        pltpu.make_async_copy(src, dst, sem.at[n])
        for n, (src, dst) in enumerate(zip(sources, results))
    ]
    for copy in copies:
        copy.start()
    for copy in copies:
        copy.wait()


def solution(mesh):
    sizes = tuple(mesh.shape[a] for a in AXES)

    def local(
        e_field,
        material,
        permittivity,
        loss,
        port_cell,
        port_owner,
        circuit_block,
        circuit_state,
        mna_update,
        mna_drive,
        mna_sense,
    ):
        slots, nodes = circuit_state.shape
        cap = slots // sizes[2]
        hbm = pl.BlockSpec(memory_space=pltpu.HBM)
        dma = pltpu.SemaphoreType.DMA
        vmem = pl.BlockSpec(memory_space=pltpu.VMEM)
        shapes = (e_field.shape, e_field.shape, circuit_state.shape)
        results = pl.pallas_call(
            functools.partial(kernel, sizes),
            out_shape=[pltpu.VMEM(shape, F32) for shape in shapes],
            in_specs=[hbm] * 11,
            out_specs=[vmem] * 3,
            scratch_shapes=[
                pltpu.SMEM(permittivity.shape, F32),
                pltpu.SMEM(loss.shape, F32),
                pltpu.SMEM(port_cell.shape, jnp.int32),
                pltpu.SMEM(port_cell.shape, jnp.int32),
                pltpu.SMEM(circuit_block.shape, jnp.int32),
                pltpu.VMEM(material.shape, jnp.int32),
                pltpu.VMEM(material.shape, F32),
                pltpu.VMEM(material.shape, F32),
                pltpu.VMEM((ITERS,) + material.shape, F32),
                pltpu.VMEM((64, 2 * ITERS * 128), F32),
                pltpu.VMEM(circuit_state.shape, F32),
                pltpu.VMEM(mna_update.shape, F32),
                pltpu.VMEM(mna_drive.shape, F32),
                pltpu.VMEM(mna_sense.shape, F32),
                pltpu.VMEM((ITERS, TILES, 8, 128), F32),
                pltpu.VMEM((ITERS, TILES, 8, 128), F32),
                pltpu.VMEM((sizes[2], cap, 128), F32),
                pltpu.VMEM((sizes[2], cap, 128), F32),
                pltpu.VMEM((sizes[2], cap, 128), F32),
                pltpu.VMEM((sizes[2], cap, 128), F32),
                pltpu.VMEM((slots, 128), F32),
                dma((11,)),
                dma((ITERS, len(MESSAGES))),
                dma((ITERS, len(MESSAGES))),
                dma((sizes[2],)),
                dma((sizes[2],)),
                dma((sizes[2],)),
                dma((sizes[2],)),
                pltpu.SemaphoreType.REGULAR,
                pltpu.SemaphoreType.REGULAR,
            ],
            compiler_params=pltpu.CompilerParams(
                collective_id=0, has_side_effects=True, vmem_limit_bytes=32 * 1024 * 1024
            ),
        )(
            *(
                pltpu.with_memory_space_constraint(array, pltpu.HBM)
                for array in (
                    e_field,
                    material,
                    permittivity,
                    loss,
                    port_cell,
                    port_owner.reshape(-1),
                    circuit_block,
                    circuit_state,
                    mna_update,
                    mna_drive,
                    mna_sense,
                )
            )
        )
        return pl.pallas_call(
            hand_out,
            out_shape=[jax.ShapeDtypeStruct(shape, F32) for shape in shapes],
            in_specs=[vmem] * 3,
            out_specs=[hbm] * 3,
            scratch_shapes=[dma((3,))],
        )(*(pltpu.with_memory_space_constraint(r, pltpu.VMEM) for r in results))

    placed = (
        P(None, "gx", "gy", "gz"),
        P("gx", "gy", "gz"),
        P(),
        P(),
        P(("gx", "gy", "gz")),
        P(("gx", "gy", "gz"), None),
        P(("gx", "gy", "gz")),
        P(("gx", "gy", "gz"), None),
        P(("gx", "gy", "gz"), None, None),
        P(("gx", "gy", "gz"), None),
        P(("gx", "gy", "gz"), None),
    )
    return jax.shard_map(
        local,
        mesh=mesh,
        in_specs=placed,
        out_specs=(
            P(None, "gx", "gy", "gz"),
            P(None, "gx", "gy", "gz"),
            P(("gx", "gy", "gz"), None),
        ),
        check_vma=False,
    )
```

```python
import functools

import jax
import jax.numpy as jnp
from jax import lax
from jax.experimental import pallas as pl
from jax.experimental.pallas import tpu as pltpu
from jax.sharding import PartitionSpec as P

ITERS = 4
MESH = pl.DeviceIdType.MESH
AXES = ("gx", "gy", "gz")
F32 = jnp.float32
BF16 = jnp.bfloat16

MESSAGES = (
    ((1, 0, -1), 0, 1, 1),
    ((-1, 0, 1), 2, 1, 1),
    ((1, 0, 0), 4, 3, 1),
    ((-1, 0, 0), 8, 2, 1),
    ((1, -1, 0), 11, 1, 1),
    ((-1, 1, 0), 13, 1, 0),
    ((0, -1, 1), 14, 1, 0),
    ((0, 1, -1), 15, 1, 0),
    ((0, 0, 1), 16, 1, 0),
    ((0, 0, -1), 17, 1, 0),
    ((0, 1, 0), 18, 3, 0),
    ((0, -1, 0), 21, 2, 0),
)
TILES = 23
LATE = (0, 1)
FAR = range(6)
LOW, HIGH, EDGES = (3,), (2,), (4, 5, 0, 1)
NEAR = range(6, 12)

def iota(shape, dim):
    return lax.broadcasted_iota(jnp.int32, shape, dim)


def full(row):
    return jnp.broadcast_to(row, (8, 128))


def split(value, parts):
    pieces = []
    for _ in range(parts):
        piece = value.astype(BF16)
        pieces.append(piece)
        value = value - piece.astype(F32)
    return pieces


def dot(a, b):
    return jnp.dot(a, b, preferred_element_type=F32)


def dot_t(a, b):
    return lax.dot_general(a, b, (((1,), (1,)), ((), ())), preferred_element_type=F32)


def kernel(
    sizes,
    e_hbm,
    mat_hbm,
    eps_hbm,
    loss_hbm,
    cell_hbm,
    owner_hbm,
    block_hbm,
    x_hbm,
    u_hbm,
    d_hbm,
    s_hbm,
    e_ref,
    h_ref,
    base_ref,
    eps_ref,
    loss_ref,
    cell_ref,
    owner_ref,
    block_ref,
    mat_ref,
    keep_ref,
    gain_ref,
    hist_ref,
    field_ref,
    x_ref,
    u_ref,
    d_ref,
    s_ref,
    send_buf,
    recv_buf,
    coef_send,
    coef_recv,
    volt_send,
    volt_recv,
    gather_buf,
    in_sem,
    send_sem,
    recv_sem,
    coef_ssem,
    coef_rsem,
    volt_ssem,
    volt_rsem,
    peers_sem,
    faces_sem,
):
    nz = sizes[2]
    cap = x_ref.shape[0] // nz
    slots = x_ref.shape[0]
    me = [lax.axis_index(a) for a in AXES]

    def exists(offset, place=me):
        ok = None
        for at, off, size in zip(place, offset, sizes):
            if off:
                one = at + off >= 0 if off < 0 else at + off < size
                ok = one if ok is None else jnp.logical_and(ok, one)
        return ok

    def device(offset):
        return tuple(at + off for at, off in zip(me, offset))

    def peer(step):
        return lax.rem(me[2] + step, nz)

    others = sorted(range(1, nz), key=lambda step: -min(step, nz - step))

    loads = [
        pltpu.make_async_copy(src, dst, in_sem.at[n])
        for n, (src, dst) in enumerate(
            (
                (e_hbm, e_ref),
                (mat_hbm, mat_ref),
                (eps_hbm, eps_ref),
                (loss_hbm, loss_ref),
                (cell_hbm, cell_ref),
                (owner_hbm, owner_ref),
                (block_hbm, block_ref),
                (u_hbm, u_ref),
                (x_hbm, x_ref),
                (d_hbm, d_ref),
                (s_hbm, s_ref),
            )
        )
    ]

    recv_buf[...] = jnp.zeros(recv_buf.shape, F32)

    barrier = pltpu.get_barrier_semaphore()
    odd = lax.rem(me[1], 2)
    is_even, is_odd = odd == 0, odd == 1
    sibling = (me[0], me[1] + 1 - 2 * odd, me[2])
    neighbours = jnp.int32(-1)
    for offset, _, _, _ in MESSAGES:
        ok = exists(offset)
        neighbours = neighbours + ok.astype(jnp.int32)
        neighbours = neighbours + exists(offset, (me[0], me[1] + 1, me[2])).astype(jnp.int32)
        if offset == (0, 1, 0):
            ok = jnp.logical_and(ok, is_odd)

        @pl.when(ok)
        def _(offset=offset):
            there = device(offset)
            pl.semaphore_signal(
                barrier,
                inc=1,
                device_id=(there[0], there[1] - lax.rem(there[1], 2), there[2]),
                device_id_type=MESH,
            )

    for step in others:
        pl.semaphore_signal(
            barrier, inc=1, device_id=(me[0], me[1] + 1 - odd, peer(step)), device_id_type=MESH
        )

    @pl.when(is_even)
    def _():
        pl.semaphore_signal(barrier, inc=1, device_id=sibling, device_id_type=MESH)

    for load in loads:
        load.start()

    row = iota((8, 128), 0)
    lane = iota((8, 128), 1)
    planes = range(8)

    for load in loads[1:7]:
        load.wait()
    mat = [mat_ref[i] for i in planes]
    keep = [jnp.zeros((8, 128), F32) for _ in planes]
    gain = [jnp.zeros((8, 128), F32) for _ in planes]
    for m in range(eps_ref.shape[0]):
        loss = jnp.full((8, 128), loss_ref[m], F32)
        eps = jnp.full((8, 128), eps_ref[m], F32)
        keep_m = (1.0 - loss) / (1.0 + loss)
        gain_m = 0.5 / (eps * (1.0 + loss))
        for i in planes:
            same = mat[i] == m
            keep[i] = jnp.where(same, keep_m, keep[i])
            gain[i] = jnp.where(same, gain_m, gain[i])
    for i in planes:
        keep_ref[i] = keep[i]
        gain_ref[i] = gain[i]

    def pack_y(c, j):
        tile = jnp.zeros((8, 128), F32)
        for i in planes:
            tile = jnp.where(row == i, full(e_ref[c, i, j : j + 1, :]), tile)
        return tile

    def pack_z(comps, k):
        tile = jnp.zeros((8, 128), F32)
        for c in comps:
            for i in planes:
                tile = jnp.where(lane == c * 8 + i, full(e_ref[c, i][:, k : k + 1]), tile)
        return tile

    def pack_tiles(n, tiles):
        for t, tile in tiles.items():
            send_buf[n, t] = tile

    def pack_low(n):
        pack_tiles(n, {8: e_ref[1, 0], 9: e_ref[2, 0]})

    def pack_high(n):
        pack_tiles(n, {4 + c: e_ref[c, 7] for c in range(3)})

    def pack_edges(n):
        e_x7 = e_ref[0, 7]
        pack_tiles(
            n,
            {
                0: pltpu.roll(e_x7, 127, 1),
                2: pltpu.roll(e_ref[2, 0], 24, 1),
                11: pltpu.roll(e_x7, 7, 0),
                13: e_ref[1, 0],
            },
        )

    def pack_gains():
        send_buf[0, 1] = pltpu.roll(gain[7], 127, 1)
        send_buf[0, 3] = pltpu.roll(gain[0], 24, 1)
        send_buf[0, 7] = gain[7]
        send_buf[0, 10] = gain[0]
        send_buf[0, 12] = pltpu.roll(gain[7], 7, 0)

    def pack_near(n):
        y7 = [pack_y(c, 7) for c in range(3)]
        z127 = pack_z((0, 1, 2), 127)
        tiles = [pltpu.roll(z127, 7, 0), pltpu.roll(y7[1], 127, 1), z127, pack_z((0, 1), 0)]
        tiles += y7 + [pack_y(0, 0), pack_y(2, 0)]
        for t, tile in enumerate(tiles):
            send_buf[n, 14 + t] = tile

    def message(m, n):
        offset, first, count, more = MESSAGES[m]
        tiles = pl.ds(first, count + (more if n == 0 else 0))
        return pltpu.make_async_remote_copy(
            src_ref=send_buf.at[n, tiles],
            dst_ref=recv_buf.at[n, tiles],
            send_sem=send_sem.at[n, m],
            recv_sem=recv_sem.at[n, m],
            device_id=device(offset),
            device_id_type=MESH,
        )

    def send(which, n):
        for m in which:

            @pl.when(exists(MESSAGES[m][0]))
            def _(m=m):
                message(m, n).start()

    def wait_recv(which, n):
        for m in which:

            @pl.when(exists(tuple(-o for o in MESSAGES[m][0])))
            def _(m=m):
                message(m, n).wait_recv()

    def wait_send(n):
        for m in range(len(MESSAGES)):

            @pl.when(exists(MESSAGES[m][0]))
            def _(m=m):
                message(m, n).wait_send()

    loads[0].wait()
    pack_low(0)
    pack_high(0)
    pack_edges(0)
    pack_gains()
    pack_near(0)

    ports = cell_ref.shape[0]
    owners = [owner_ref[q] for q in range(ports)]
    srow = iota((slots, 128), 0)
    slane = iota((slots, 128), 1)
    slot_cell = jnp.full((slots, 128), -1, jnp.int32)
    lane_cell = jnp.full((8, 128), -1, jnp.int32)
    for q in range(ports):
        index = owners[q] * cap
        for r in range(q):
            index = index + jnp.where(owners[r] == owners[q], 1, 0)
        slot_cell = jnp.where(srow == index, cell_ref[q], slot_cell)
        lane_cell = jnp.where(lax.rem(lane, slots) == index, cell_ref[q], lane_cell)
    in_lane = jnp.logical_and(slot_cell >= 0, (slot_cell & 127) == slane)
    gather = jnp.where((slot_cell >> 7) == lax.rem(slane, 64), 1.0, 0.0).astype(BF16)
    in_row = jnp.broadcast_to((lane_cell >> 7)[0:1, :], (64, 128))
    scatter = jnp.where(in_row == iota((64, 128), 0), 1.0, 0.0).astype(BF16)

    for load in loads[7:]:
        load.wait()
    brow = iota((slots + 8, 128), 0)
    which = jnp.where(brow == slots + 1, 1, 0)
    for s in range(slots):
        which = jnp.where(brow == s, block_ref[s], which)
    first = jnp.concatenate([which, which], axis=1) == 0
    nodes = x_ref.shape[1]
    state = jnp.concatenate(
        [x_ref[...], d_ref[...], jnp.zeros((6, nodes), F32)], axis=0
    )
    sense = jnp.where(
        first,
        jnp.broadcast_to(s_ref[0:1, :], first.shape),
        jnp.broadcast_to(s_ref[1:2, :], first.shape),
    )
    halves = [split(u_ref[b], 2) for b in range(2)]
    drives = [state[slots : slots + 2]]
    readouts = [jnp.sum(state * sense, axis=1, keepdims=True)]
    for n in range(ITERS):
        hi, lo = split(state, 2)
        both = [
            dot_t(hi, high) + (dot_t(hi, low) + dot_t(lo, high)) for high, low in halves
        ]
        state = jnp.where(first, both[0], both[1])
        readouts.append(jnp.sum(state * sense, axis=1, keepdims=True))
        if n < ITERS - 1:
            drives.append(state[slots : slots + 2])
    base_ref[...] = state[:slots]
    is_first = first[:slots, :128]
    coefs = jnp.zeros((slots, 128), F32)
    for n in range(ITERS):
        coefs = jnp.where(slane == n, readouts[n + 1][:slots], coefs)
        kick = jnp.where(is_first, readouts[n][slots : slots + 1], readouts[n][slots + 1 : slots + 2])
        coefs = jnp.where(slane == ITERS + n, kick, coefs)
    for g in range(nz):
        coef_send[g] = coefs[g * cap : (g + 1) * cap]

    def exchange(step, src, dst, ssem, rsem):
        there = peer(step)
        return pltpu.make_async_remote_copy(
            src_ref=src.at[there],
            dst_ref=dst.at[me[2]],
            send_sem=ssem.at[step],
            recv_sem=rsem.at[step],
            device_id=(me[0], me[1], there),
            device_id_type=MESH,
        )

    coef_copies = [
        exchange(step, coef_send, coef_recv, coef_ssem, coef_rsem) for step in others
    ]
    coef_recv[me[2]] = coef_send[me[2]]

    def start_circuits():
        @pl.when(is_odd)
        def _():
            pl.semaphore_wait(barrier, 2 * (nz - 1) + 1)
            pl.semaphore_signal(peers_sem, inc=1, device_id=sibling, device_id_type=MESH)

        @pl.when(is_even)
        def _():
            pl.semaphore_wait(peers_sem, 1)

        for copy in coef_copies:
            copy.start()

    def start_faces():
        @pl.when(is_even)
        def _():
            pl.semaphore_wait(barrier, neighbours)
            pl.semaphore_signal(faces_sem, inc=1, device_id=sibling, device_id_type=MESH)

        @pl.when(is_odd)
        def _():
            pl.semaphore_wait(faces_sem, 1)

        send(LOW + HIGH + EDGES, 0)
        send(NEAR, 0)

    last = me[2] >= nz - 4
    pl.when(last)(start_circuits)
    start_faces()
    pl.when(jnp.logical_not(last))(start_circuits)

    low = [jnp.where(me[d] > 0, 1.0, 0.0).astype(F32) for d in range(3)]
    ghosts = None
    owed = None
    volts = []

    def lacking(where, tile, value):
        return jnp.where(where, 0.5 * recv_buf[0, tile], 0.0) * value

    def voltages(n):
        e_z = [e_ref[2, i] for i in planes]
        for i in planes:
            hist_ref[n, i] = e_z[i]
        stack = jnp.concatenate(e_z, axis=0)
        found = dot(gather, jnp.concatenate(split(stack, 2), axis=0))
        volts.append(jnp.sum(jnp.where(in_lane, found, 0.0), axis=1, keepdims=True))

    def send_voltages():
        tile = jnp.zeros((slots, 128), F32)
        for k in range(ITERS):
            tile = jnp.where(slane == k, volts[k], tile)
        for g in range(nz):
            volt_send[g] = tile[g * cap : (g + 1) * cap]
        copies = [exchange(step, volt_send, volt_recv, volt_ssem, volt_rsem) for step in others]
        for copy in copies:
            copy.start()
        volt_recv[me[2]] = volt_send[me[2]]
        return copies

    def fields(table, ks):
        spread = jnp.concatenate(
            [
                jnp.where(in_lane, jnp.broadcast_to(table[:, k : k + 1], (slots, 128)), 0.0)
                for k in ks
            ],
            axis=1,
        )
        pieces = split(spread, 3) + [jnp.zeros(spread.shape, BF16)]
        found = dot(scatter, jnp.concatenate(pieces, axis=0))
        for at, k in enumerate(ks):
            field_ref[:, 128 * k : 128 * (k + 1)] = found[:, 128 * at : 128 * (at + 1)]

    voltages(0)
    for n in range(ITERS):
        if n == ITERS - 1 and n == 0:
            volt_copies = send_voltages()

        def got(t, n=n):
            return recv_buf[n, t]

        wait_recv(NEAR, n)

        fx_m, fy_m, fz_m = got(18), got(19), got(20)
        fx_0, fz_0 = send_buf[n, 21], send_buf[n, 22]
        fy_k = jnp.where(lane == 127, got(15), pltpu.roll(fy_m, 127, 1))
        hx_y = -0.5 * ((fz_0 - fz_m) - (fy_k - fy_m)) * low[1]
        fy_i = jnp.where(row == 7, 0.0, pltpu.roll(fy_m, 7, 0))
        hz_y = -0.5 * ((fy_i - fy_m) - (fx_0 - fx_m)) * low[1]
        g_m, g_0, g_edge = got(16), send_buf[n, 17], got(14)
        gz_j = jnp.where(row == 7, g_edge, pltpu.roll(g_m, 7, 0)) - g_m
        gz_i = jnp.where(lane == 23, 0.0, pltpu.roll(g_m, 127, 1)) - g_m
        g_d = g_0 - g_m
        h_z = -0.5 * low[2] * jnp.where(
            lane < 8, g_d - pltpu.roll(gz_i, 128 - 16, 1), pltpu.roll(gz_j, 128 - 8, 1) - g_d
        )
        if n > 0:
            hx_y, hz_y, h_z = hx_y + ghosts[2], hz_y + ghosts[3], h_z + ghosts[4]

        zp = got(17)
        was_owed = owed
        owed = [None] * 5
        if n < ITERS - 1:
            owed[3:] = [e_ref[2, 0], pltpu.roll(e_ref[0, 7], 23, 1)]

        def update_h(i, ey_i, ez_i, which, n=n, zp=zp):
            ex, ey, ez = e_ref[0, i], e_ref[1, i], e_ref[2, i]
            if 0 in which:
                ez_j = jnp.where(
                    row == 7, full(recv_buf[n, 22, i : i + 1, :]), pltpu.roll(ez, 7, 0)
                )
                ey_k = jnp.where(lane == 127, full(zp[:, 8 + i : 9 + i]), pltpu.roll(ey, 127, 1))
                hx = -0.5 * ((ez_j - ez) - (ey_k - ey))
                h_ref[0, i] = hx if n == 0 else h_ref[0, i] + hx
            if 1 in which:
                ex_j = jnp.where(
                    row == 7, full(recv_buf[n, 21, i : i + 1, :]), pltpu.roll(ex, 7, 0)
                )
                ex_k = jnp.where(lane == 127, full(zp[:, i : i + 1]), pltpu.roll(ex, 127, 1))
                hy = -0.5 * ((ex_k - ex) - (ez_i - ez))
                hz = -0.5 * ((ey_i - ey) - (ex_j - ex))
                h_ref[1, i] = hy if n == 0 else h_ref[1, i] + hy
                h_ref[2, i] = hz if n == 0 else h_ref[2, i] + hz

        def update_e(i, hy_i, hz_i, hx_y, hz_y, h_z, n=n):
            hx, hy, hz = h_ref[0, i], h_ref[1, i], h_ref[2, i]
            hx_j = jnp.where(row == 0, full(hx_y[i : i + 1, :]), pltpu.roll(hx, 1, 0))
            hz_j = jnp.where(row == 0, full(hz_y[i : i + 1, :]), pltpu.roll(hz, 1, 0))
            hy_k = jnp.where(lane == 0, full(h_z[:, i : i + 1]), pltpu.roll(hy, 1, 1))
            hx_k = jnp.where(lane == 0, full(h_z[:, 8 + i : 9 + i]), pltpu.roll(hx, 1, 1))
            rows = slice(8 * i, 8 * i + 8)
            current = field_ref[rows, 128 * n : 128 * (n + 1)]
            for k in range(n + 1):
                at = ITERS + n - k
                current = current + field_ref[rows, 128 * at : 128 * (at + 1)] * hist_ref[k, i]
            keep_i, gain_i = keep_ref[i], gain_ref[i]
            e_ref[0, i] = keep_i * e_ref[0, i] + gain_i * ((hz - hz_j) - (hy - hy_k))
            e_ref[1, i] = keep_i * e_ref[1, i] + gain_i * ((hx - hx_k) - (hz - hz_i))
            e_ref[2, i] = keep_i * e_ref[2, i] + gain_i * (((hy - hy_i) - (hx - hx_j)) - current)

        for i in range(7):
            update_h(i, e_ref[1, i + 1], e_ref[2, i + 1], (0, 1))
        update_h(7, None, None, (0,))
        if n == 0:
            for copy in coef_copies:
                copy.wait_recv()
            for g in range(nz):
                gather_buf[g * cap : (g + 1) * cap, :] = coef_recv[g]
            fields(gather_buf[...], [0, ITERS])
        e_0 = [e_ref[c, 0] for c in range(3)]
        def inner(n=n, hx_y=hx_y, hz_y=hz_y, h_z=h_z):
            for i in range(1, 7):
                update_e(i, h_ref[1, i - 1], h_ref[2, i - 1], hx_y, hz_y, h_z)

        if n > 0:
            inner()

        wait_recv([m for m in FAR if m not in LATE], n)
        ex_m, ey_m, ez_m = got(4), got(5), got(6)
        ey_p, ez_p = got(8), got(9)
        ex_edge = got(11)
        if n > 0:
            ex_m, ez_p, ex_edge = ex_m + was_owed[0], ez_p + was_owed[1], ex_edge + was_owed[2]
        ex_k = jnp.where(lane == 127, 0.0, pltpu.roll(ex_m, 127, 1))
        ex_j = jnp.where(row == 7, ex_edge, pltpu.roll(ex_m, 7, 0))
        hy_x = -0.5 * ((ex_k - ex_m) - (e_0[2] - ez_m)) * low[0]
        hz_x = -0.5 * ((e_0[1] - ey_m) - (ex_j - ex_m)) * low[0]
        if n > 0:
            hy_x, hz_x = hy_x + ghosts[0], hz_x + ghosts[1]
        update_e(0, hy_x, hz_x, hx_y, hz_y, h_z)
        if n < ITERS - 1:
            pack_low(n + 1)
            send(LOW, n + 1)
        update_h(7, ey_p, ez_p, (1,))
        hz_y = hz_y - jnp.where(row == 7, 0.5 * low[1] * got(13), 0.0)
        ghosts = [hy_x, hz_x, hx_y, hz_y, h_z]
        update_e(7, h_ref[1, 6], h_ref[2, 6], hx_y, hz_y, h_z)

        if n < ITERS - 1:
            pack_high(n + 1)
            send(HIGH, n + 1)
            pack_edges(n + 1)
            send(EDGES, n + 1)
            owed[:3] = [
                lacking(lane == 0, 7, pltpu.roll(g_m, 112, 1)),
                lacking(lane == 127, 10, pltpu.roll(zp, 120, 1)),
                lacking(jnp.logical_and(lane == 0, row == 7), 12, pltpu.roll(g_edge, 112, 1)),
            ]
        if n == 0:
            inner()
        if n == 0 and ITERS > 1:
            fields(gather_buf[...], [k for k in range(2 * ITERS) if k not in (0, ITERS)])

        wait_recv(LATE, n)
        x_edge, z_edge = got(0), got(2)
        if n > 0:
            x_edge = x_edge + lacking(lane == 127, 1, was_owed[3])
            z_edge = z_edge + lacking(lane == 23, 3, was_owed[4])
        x_edge = jnp.where(lane == 127, 0.5 * low[0] * x_edge, 0.0)
        z_edge = jnp.where(lane == 23, 0.5 * low[2] * z_edge, 0.0)
        ghosts[0] = ghosts[0] - x_edge
        ghosts[4] = ghosts[4] + pltpu.roll(z_edge, 112, 1)
        e_ref[2, 0] = e_ref[2, 0] + gain_ref[0] * x_edge
        e_ref[0, 7] = e_ref[0, 7] + gain_ref[7] * pltpu.roll(z_edge, 105, 1)

        if n < ITERS - 1:
            if n == ITERS - 2:
                voltages(n + 1)
                volt_copies = send_voltages()
            pack_near(n + 1)
            send(NEAR, n + 1)
            if n < ITERS - 2:
                voltages(n + 1)

    final = base_ref[...]
    pick = first[:slots]
    rows = [
        jnp.where(
            pick,
            jnp.broadcast_to(drive[0:1], final.shape),
            jnp.broadcast_to(drive[1:2], final.shape),
        )
        for drive in reversed(drives)
    ]
    for copy in volt_copies:
        copy.wait_recv()
    for g in range(nz):
        gather_buf[g * cap : (g + 1) * cap, :] = volt_recv[g]
    table = gather_buf[...]
    for k in range(ITERS):
        final = final + rows[k] * table[:, k : k + 1]
    base_ref[...] = final
    for copy in coef_copies + volt_copies:
        copy.wait_send()
    for n in range(ITERS):
        wait_send(n)


def hand_out(*refs):
    sources, results, sem = refs[:3], refs[3:6], refs[6]
    copies = [
        pltpu.make_async_copy(src, dst, sem.at[n])
        for n, (src, dst) in enumerate(zip(sources, results))
    ]
    for copy in copies:
        copy.start()
    for copy in copies:
        copy.wait()


def solution(mesh):
    sizes = tuple(mesh.shape[a] for a in AXES)

    def local(
        e_field,
        material,
        permittivity,
        loss,
        port_cell,
        port_owner,
        circuit_block,
        circuit_state,
        mna_update,
        mna_drive,
        mna_sense,
    ):
        slots, nodes = circuit_state.shape
        cap = slots // sizes[2]
        hbm = pl.BlockSpec(memory_space=pltpu.HBM)
        dma = pltpu.SemaphoreType.DMA
        vmem = pl.BlockSpec(memory_space=pltpu.VMEM)
        shapes = (e_field.shape, e_field.shape, circuit_state.shape)
        results = pl.pallas_call(
            functools.partial(kernel, sizes),
            out_shape=[pltpu.VMEM(shape, F32) for shape in shapes],
            in_specs=[hbm] * 11,
            out_specs=[vmem] * 3,
            scratch_shapes=[
                pltpu.SMEM(permittivity.shape, F32),
                pltpu.SMEM(loss.shape, F32),
                pltpu.SMEM(port_cell.shape, jnp.int32),
                pltpu.SMEM(port_cell.shape, jnp.int32),
                pltpu.SMEM(circuit_block.shape, jnp.int32),
                pltpu.VMEM(material.shape, jnp.int32),
                pltpu.VMEM(material.shape, F32),
                pltpu.VMEM(material.shape, F32),
                pltpu.VMEM((ITERS,) + material.shape, F32),
                pltpu.VMEM((64, 2 * ITERS * 128), F32),
                pltpu.VMEM(circuit_state.shape, F32),
                pltpu.VMEM(mna_update.shape, F32),
                pltpu.VMEM(mna_drive.shape, F32),
                pltpu.VMEM(mna_sense.shape, F32),
                pltpu.VMEM((ITERS, TILES, 8, 128), F32),
                pltpu.VMEM((ITERS, TILES, 8, 128), F32),
                pltpu.VMEM((sizes[2], cap, 128), F32),
                pltpu.VMEM((sizes[2], cap, 128), F32),
                pltpu.VMEM((sizes[2], cap, 128), F32),
                pltpu.VMEM((sizes[2], cap, 128), F32),
                pltpu.VMEM((slots, 128), F32),
                dma((11,)),
                dma((ITERS, len(MESSAGES))),
                dma((ITERS, len(MESSAGES))),
                dma((sizes[2],)),
                dma((sizes[2],)),
                dma((sizes[2],)),
                dma((sizes[2],)),
                pltpu.SemaphoreType.REGULAR,
                pltpu.SemaphoreType.REGULAR,
            ],
            compiler_params=pltpu.CompilerParams(
                collective_id=0, has_side_effects=True, vmem_limit_bytes=32 * 1024 * 1024
            ),
        )(
            *(
                pltpu.with_memory_space_constraint(array, pltpu.HBM)
                for array in (
                    e_field,
                    material,
                    permittivity,
                    loss,
                    port_cell,
                    port_owner.reshape(-1),
                    circuit_block,
                    circuit_state,
                    mna_update,
                    mna_drive,
                    mna_sense,
                )
            )
        )
        return pl.pallas_call(
            hand_out,
            out_shape=[jax.ShapeDtypeStruct(shape, F32) for shape in shapes],
            in_specs=[vmem] * 3,
            out_specs=[hbm] * 3,
            scratch_shapes=[dma((3,))],
        )(*(pltpu.with_memory_space_constraint(r, pltpu.VMEM) for r in results))

    placed = (
        P(None, "gx", "gy", "gz"),
        P("gx", "gy", "gz"),
        P(),
        P(),
        P(("gx", "gy", "gz")),
        P(("gx", "gy", "gz"), None),
        P(("gx", "gy", "gz")),
        P(("gx", "gy", "gz"), None),
        P(("gx", "gy", "gz"), None, None),
        P(("gx", "gy", "gz"), None),
        P(("gx", "gy", "gz"), None),
    )
    return jax.shard_map(
        local,
        mesh=mesh,
        in_specs=placed,
        out_specs=(
            P(None, "gx", "gy", "gz"),
            P(None, "gx", "gy", "gz"),
            P(("gx", "gy", "gz"), None),
        ),
        check_vma=False,
    )
```

```python
import functools

import jax
import jax.numpy as jnp
from jax import lax
from jax.experimental import pallas as pl
from jax.experimental.pallas import tpu as pltpu
from jax.sharding import PartitionSpec as P

ITERS = 4
MESH = pl.DeviceIdType.MESH
AXES = ("gx", "gy", "gz")
F32 = jnp.float32
BF16 = jnp.bfloat16

MESSAGES = (
    ((1, 0, -1), 0, 1, 1),
    ((-1, 0, 1), 2, 1, 1),
    ((1, 0, 0), 4, 3, 1),
    ((-1, 0, 0), 8, 2, 1),
    ((1, -1, 0), 11, 1, 1),
    ((-1, 1, 0), 13, 1, 0),
    ((0, -1, 1), 14, 1, 0),
    ((0, 1, -1), 15, 1, 0),
    ((0, 0, 1), 16, 1, 0),
    ((0, 0, -1), 17, 1, 0),
    ((0, 1, 0), 18, 3, 0),
    ((0, -1, 0), 21, 2, 0),
)
TILES = 23
LATE = (0, 1)
FAR = range(6)
LOW, HIGH, EDGES = (3,), (2,), (4, 5, 0, 1)
NEAR = range(6, 12)

def iota(shape, dim):
    return lax.broadcasted_iota(jnp.int32, shape, dim)


def full(row):
    return jnp.broadcast_to(row, (8, 128))


def split(value, parts):
    pieces = []
    for _ in range(parts):
        piece = value.astype(BF16)
        pieces.append(piece)
        value = value - piece.astype(F32)
    return pieces


def dot(a, b):
    return jnp.dot(a, b, preferred_element_type=F32)


def dot_t(a, b):
    return lax.dot_general(a, b, (((1,), (1,)), ((), ())), preferred_element_type=F32)


def kernel(
    sizes,
    e_hbm,
    mat_hbm,
    eps_hbm,
    loss_hbm,
    cell_hbm,
    owner_hbm,
    block_hbm,
    x_hbm,
    u_hbm,
    d_hbm,
    s_hbm,
    e_ref,
    h_ref,
    base_ref,
    eps_ref,
    loss_ref,
    cell_ref,
    owner_ref,
    block_ref,
    mat_ref,
    keep_ref,
    gain_ref,
    hist_ref,
    field_ref,
    x_ref,
    u_ref,
    d_ref,
    s_ref,
    send_buf,
    recv_buf,
    coef_send,
    coef_recv,
    volt_send,
    volt_recv,
    gather_buf,
    in_sem,
    send_sem,
    recv_sem,
    coef_ssem,
    coef_rsem,
    volt_ssem,
    volt_rsem,
    peers_sem,
    faces_sem,
):
    nz = sizes[2]
    cap = x_ref.shape[0] // nz
    slots = x_ref.shape[0]
    me = [lax.axis_index(a) for a in AXES]

    def exists(offset, place=me):
        ok = None
        for at, off, size in zip(place, offset, sizes):
            if off:
                one = at + off >= 0 if off < 0 else at + off < size
                ok = one if ok is None else jnp.logical_and(ok, one)
        return ok

    def device(offset):
        return tuple(at + off for at, off in zip(me, offset))

    def peer(step):
        return lax.rem(me[2] + step, nz)

    others = sorted(range(1, nz), key=lambda step: -min(step, nz - step))

    loads = [
        pltpu.make_async_copy(src, dst, in_sem.at[n])
        for n, (src, dst) in enumerate(
            (
                (e_hbm, e_ref),
                (mat_hbm, mat_ref),
                (eps_hbm, eps_ref),
                (loss_hbm, loss_ref),
                (cell_hbm, cell_ref),
                (owner_hbm, owner_ref),
                (block_hbm, block_ref),
                (u_hbm, u_ref),
                (x_hbm, x_ref),
                (d_hbm, d_ref),
                (s_hbm, s_ref),
            )
        )
    ]

    barrier = pltpu.get_barrier_semaphore()
    odd = lax.rem(me[1], 2)
    is_even, is_odd = odd == 0, odd == 1
    sibling = (me[0], me[1] + 1 - 2 * odd, me[2])
    for step in others:
        pl.semaphore_signal(
            barrier, inc=1, device_id=(me[0], me[1] + 1 - odd, peer(step)), device_id_type=MESH
        )

    recv_buf[...] = jnp.zeros(recv_buf.shape, F32)
    neighbours = jnp.int32(-1)
    for offset, _, _, _ in MESSAGES:
        ok = exists(offset)
        neighbours = neighbours + ok.astype(jnp.int32)
        neighbours = neighbours + exists(offset, (me[0], me[1] + 1, me[2])).astype(jnp.int32)
        if offset == (0, 1, 0):
            ok = jnp.logical_and(ok, is_odd)

        @pl.when(ok)
        def _(offset=offset):
            there = device(offset)
            pl.semaphore_signal(
                barrier,
                inc=1,
                device_id=(there[0], there[1] - lax.rem(there[1], 2), there[2]),
                device_id_type=MESH,
            )

    @pl.when(is_even)
    def _():
        pl.semaphore_signal(barrier, inc=1, device_id=sibling, device_id_type=MESH)

    for load in loads:
        load.start()

    row = iota((8, 128), 0)
    lane = iota((8, 128), 1)
    planes = range(8)

    for load in loads[1:7]:
        load.wait()
    mat = [mat_ref[i] for i in planes]
    keep = [jnp.zeros((8, 128), F32) for _ in planes]
    gain = [jnp.zeros((8, 128), F32) for _ in planes]
    for m in range(eps_ref.shape[0]):
        loss = jnp.full((8, 128), loss_ref[m], F32)
        eps = jnp.full((8, 128), eps_ref[m], F32)
        keep_m = (1.0 - loss) / (1.0 + loss)
        gain_m = 0.5 / (eps * (1.0 + loss))
        for i in planes:
            same = mat[i] == m
            keep[i] = jnp.where(same, keep_m, keep[i])
            gain[i] = jnp.where(same, gain_m, gain[i])
    for i in planes:
        keep_ref[i] = keep[i]
        gain_ref[i] = gain[i]

    def pack_y(c, j):
        tile = jnp.zeros((8, 128), F32)
        for i in planes:
            tile = jnp.where(row == i, full(e_ref[c, i, j : j + 1, :]), tile)
        return tile

    def pack_z(comps, k):
        tile = jnp.zeros((8, 128), F32)
        for c in comps:
            for i in planes:
                tile = jnp.where(lane == c * 8 + i, full(e_ref[c, i][:, k : k + 1]), tile)
        return tile

    def pack_tiles(n, tiles):
        for t, tile in tiles.items():
            send_buf[n, t] = tile

    def pack_low(n):
        pack_tiles(n, {8: e_ref[1, 0], 9: e_ref[2, 0]})

    def pack_high(n):
        pack_tiles(n, {4 + c: e_ref[c, 7] for c in range(3)})

    def pack_edges(n):
        e_x7 = e_ref[0, 7]
        pack_tiles(
            n,
            {
                0: pltpu.roll(e_x7, 127, 1),
                2: pltpu.roll(e_ref[2, 0], 24, 1),
                11: pltpu.roll(e_x7, 7, 0),
                13: e_ref[1, 0],
            },
        )

    def pack_gains():
        send_buf[0, 1] = pltpu.roll(gain[7], 127, 1)
        send_buf[0, 3] = pltpu.roll(gain[0], 24, 1)
        send_buf[0, 7] = gain[7]
        send_buf[0, 10] = gain[0]
        send_buf[0, 12] = pltpu.roll(gain[7], 7, 0)

    def pack_near(n):
        y7 = [pack_y(c, 7) for c in range(3)]
        z127 = pack_z((0, 1, 2), 127)
        tiles = [pltpu.roll(z127, 7, 0), pltpu.roll(y7[1], 127, 1), z127, pack_z((0, 1), 0)]
        tiles += y7 + [pack_y(0, 0), pack_y(2, 0)]
        for t, tile in enumerate(tiles):
            send_buf[n, 14 + t] = tile

    def message(m, n):
        offset, first, count, more = MESSAGES[m]
        tiles = pl.ds(first, count + (more if n == 0 else 0))
        return pltpu.make_async_remote_copy(
            src_ref=send_buf.at[n, tiles],
            dst_ref=recv_buf.at[n, tiles],
            send_sem=send_sem.at[n, m],
            recv_sem=recv_sem.at[n, m],
            device_id=device(offset),
            device_id_type=MESH,
        )

    def send(which, n):
        for m in which:

            @pl.when(exists(MESSAGES[m][0]))
            def _(m=m):
                message(m, n).start()

    def wait_recv(which, n):
        for m in which:

            @pl.when(exists(tuple(-o for o in MESSAGES[m][0])))
            def _(m=m):
                message(m, n).wait_recv()

    def wait_send(n):
        for m in range(len(MESSAGES)):

            @pl.when(exists(MESSAGES[m][0]))
            def _(m=m):
                message(m, n).wait_send()

    loads[0].wait()
    pack_low(0)
    pack_high(0)
    pack_edges(0)
    pack_gains()
    pack_near(0)

    ports = cell_ref.shape[0]
    owners = [owner_ref[q] for q in range(ports)]
    srow = iota((slots, 128), 0)
    slane = iota((slots, 128), 1)
    slot_cell = jnp.full((slots, 128), -1, jnp.int32)
    lane_cell = jnp.full((8, 128), -1, jnp.int32)
    for q in range(ports):
        index = owners[q] * cap
        for r in range(q):
            index = index + jnp.where(owners[r] == owners[q], 1, 0)
        slot_cell = jnp.where(srow == index, cell_ref[q], slot_cell)
        lane_cell = jnp.where(lax.rem(lane, slots) == index, cell_ref[q], lane_cell)
    in_lane = jnp.logical_and(slot_cell >= 0, (slot_cell & 127) == slane)
    gather = jnp.where((slot_cell >> 7) == lax.rem(slane, 64), 1.0, 0.0).astype(BF16)
    in_row = jnp.broadcast_to((lane_cell >> 7)[0:1, :], (64, 128))
    scatter = jnp.where(in_row == iota((64, 128), 0), 1.0, 0.0).astype(BF16)

    for load in loads[7:]:
        load.wait()
    brow = iota((slots + 8, 128), 0)
    which = jnp.where(brow == slots + 1, 1, 0)
    for s in range(slots):
        which = jnp.where(brow == s, block_ref[s], which)
    first = jnp.concatenate([which, which], axis=1) == 0
    nodes = x_ref.shape[1]
    state = jnp.concatenate(
        [x_ref[...], d_ref[...], jnp.zeros((6, nodes), F32)], axis=0
    )
    sense = jnp.where(
        first,
        jnp.broadcast_to(s_ref[0:1, :], first.shape),
        jnp.broadcast_to(s_ref[1:2, :], first.shape),
    )
    halves = [split(u_ref[b], 2) for b in range(2)]
    drives = [state[slots : slots + 2]]
    readouts = [jnp.sum(state * sense, axis=1, keepdims=True)]
    for n in range(ITERS):
        hi, lo = split(state, 2)
        both = [
            dot_t(hi, high) + (dot_t(hi, low) + dot_t(lo, high)) for high, low in halves
        ]
        state = jnp.where(first, both[0], both[1])
        readouts.append(jnp.sum(state * sense, axis=1, keepdims=True))
        if n < ITERS - 1:
            drives.append(state[slots : slots + 2])
    base_ref[...] = state[:slots]
    is_first = first[:slots, :128]
    coefs = jnp.zeros((slots, 128), F32)
    for n in range(ITERS):
        coefs = jnp.where(slane == n, readouts[n + 1][:slots], coefs)
        kick = jnp.where(is_first, readouts[n][slots : slots + 1], readouts[n][slots + 1 : slots + 2])
        coefs = jnp.where(slane == ITERS + n, kick, coefs)
    for g in range(nz):
        coef_send[g] = coefs[g * cap : (g + 1) * cap]

    def exchange(step, src, dst, ssem, rsem):
        there = peer(step)
        return pltpu.make_async_remote_copy(
            src_ref=src.at[there],
            dst_ref=dst.at[me[2]],
            send_sem=ssem.at[step],
            recv_sem=rsem.at[step],
            device_id=(me[0], me[1], there),
            device_id_type=MESH,
        )

    coef_copies = [
        exchange(step, coef_send, coef_recv, coef_ssem, coef_rsem) for step in others
    ]
    coef_recv[me[2]] = coef_send[me[2]]

    def start_circuits():
        @pl.when(is_odd)
        def _():
            pl.semaphore_wait(barrier, 2 * (nz - 1) + 1)
            pl.semaphore_signal(peers_sem, inc=1, device_id=sibling, device_id_type=MESH)

        @pl.when(is_even)
        def _():
            pl.semaphore_wait(peers_sem, 1)

        for copy in coef_copies:
            copy.start()

    def start_faces():
        @pl.when(is_even)
        def _():
            pl.semaphore_wait(barrier, neighbours)
            pl.semaphore_signal(faces_sem, inc=1, device_id=sibling, device_id_type=MESH)

        @pl.when(is_odd)
        def _():
            pl.semaphore_wait(faces_sem, 1)

        send(LOW + HIGH + EDGES, 0)
        send(NEAR, 0)

    last = me[2] >= nz - 4
    pl.when(last)(start_circuits)
    start_faces()
    pl.when(jnp.logical_not(last))(start_circuits)

    low = [jnp.where(me[d] > 0, 1.0, 0.0).astype(F32) for d in range(3)]
    ghosts = None
    owed = None
    volts = []

    def lacking(where, tile, value):
        return jnp.where(where, 0.5 * recv_buf[0, tile], 0.0) * value

    def voltages(n):
        e_z = [e_ref[2, i] for i in planes]
        for i in planes:
            hist_ref[n, i] = e_z[i]
        stack = jnp.concatenate(e_z, axis=0)
        found = dot(gather, jnp.concatenate(split(stack, 2), axis=0))
        volts.append(jnp.sum(jnp.where(in_lane, found, 0.0), axis=1, keepdims=True))

    def send_voltages():
        tile = jnp.zeros((slots, 128), F32)
        for k in range(ITERS):
            tile = jnp.where(slane == k, volts[k], tile)
        for g in range(nz):
            volt_send[g] = tile[g * cap : (g + 1) * cap]
        copies = [exchange(step, volt_send, volt_recv, volt_ssem, volt_rsem) for step in others]
        for copy in copies:
            copy.start()
        volt_recv[me[2]] = volt_send[me[2]]
        return copies

    def fields(table, ks):
        spread = jnp.concatenate(
            [
                jnp.where(in_lane, jnp.broadcast_to(table[:, k : k + 1], (slots, 128)), 0.0)
                for k in ks
            ],
            axis=1,
        )
        pieces = split(spread, 3) + [jnp.zeros(spread.shape, BF16)]
        found = dot(scatter, jnp.concatenate(pieces, axis=0))
        for at, k in enumerate(ks):
            field_ref[:, 128 * k : 128 * (k + 1)] = found[:, 128 * at : 128 * (at + 1)]

    voltages(0)
    for n in range(ITERS):
        if n == ITERS - 1 and n == 0:
            volt_copies = send_voltages()

        def got(t, n=n):
            return recv_buf[n, t]

        wait_recv(NEAR, n)

        fx_m, fy_m, fz_m = got(18), got(19), got(20)
        fx_0, fz_0 = send_buf[n, 21], send_buf[n, 22]
        fy_k = jnp.where(lane == 127, got(15), pltpu.roll(fy_m, 127, 1))
        hx_y = -0.5 * ((fz_0 - fz_m) - (fy_k - fy_m)) * low[1]
        fy_i = jnp.where(row == 7, 0.0, pltpu.roll(fy_m, 7, 0))
        hz_y = -0.5 * ((fy_i - fy_m) - (fx_0 - fx_m)) * low[1]
        g_m, g_0, g_edge = got(16), send_buf[n, 17], got(14)
        gz_j = jnp.where(row == 7, g_edge, pltpu.roll(g_m, 7, 0)) - g_m
        gz_i = jnp.where(lane == 23, 0.0, pltpu.roll(g_m, 127, 1)) - g_m
        g_d = g_0 - g_m
        h_z = -0.5 * low[2] * jnp.where(
            lane < 8, g_d - pltpu.roll(gz_i, 128 - 16, 1), pltpu.roll(gz_j, 128 - 8, 1) - g_d
        )
        if n > 0:
            hx_y, hz_y, h_z = hx_y + ghosts[2], hz_y + ghosts[3], h_z + ghosts[4]

        zp = got(17)
        was_owed = owed
        owed = [None] * 5
        if n < ITERS - 1:
            owed[3:] = [e_ref[2, 0], pltpu.roll(e_ref[0, 7], 23, 1)]

        def update_h(i, ey_i, ez_i, which, n=n, zp=zp):
            ex, ey, ez = e_ref[0, i], e_ref[1, i], e_ref[2, i]
            if 0 in which:
                ez_j = jnp.where(
                    row == 7, full(recv_buf[n, 22, i : i + 1, :]), pltpu.roll(ez, 7, 0)
                )
                ey_k = jnp.where(lane == 127, full(zp[:, 8 + i : 9 + i]), pltpu.roll(ey, 127, 1))
                hx = -0.5 * ((ez_j - ez) - (ey_k - ey))
                h_ref[0, i] = hx if n == 0 else h_ref[0, i] + hx
            if 1 in which:
                ex_j = jnp.where(
                    row == 7, full(recv_buf[n, 21, i : i + 1, :]), pltpu.roll(ex, 7, 0)
                )
                ex_k = jnp.where(lane == 127, full(zp[:, i : i + 1]), pltpu.roll(ex, 127, 1))
                hy = -0.5 * ((ex_k - ex) - (ez_i - ez))
                hz = -0.5 * ((ey_i - ey) - (ex_j - ex))
                h_ref[1, i] = hy if n == 0 else h_ref[1, i] + hy
                h_ref[2, i] = hz if n == 0 else h_ref[2, i] + hz

        def update_e(i, hy_i, hz_i, hx_y, hz_y, h_z, n=n):
            hx, hy, hz = h_ref[0, i], h_ref[1, i], h_ref[2, i]
            hx_j = jnp.where(row == 0, full(hx_y[i : i + 1, :]), pltpu.roll(hx, 1, 0))
            hz_j = jnp.where(row == 0, full(hz_y[i : i + 1, :]), pltpu.roll(hz, 1, 0))
            hy_k = jnp.where(lane == 0, full(h_z[:, i : i + 1]), pltpu.roll(hy, 1, 1))
            hx_k = jnp.where(lane == 0, full(h_z[:, 8 + i : 9 + i]), pltpu.roll(hx, 1, 1))
            rows = slice(8 * i, 8 * i + 8)
            current = field_ref[rows, 128 * n : 128 * (n + 1)]
            for k in range(n + 1):
                at = ITERS + n - k
                current = current + field_ref[rows, 128 * at : 128 * (at + 1)] * hist_ref[k, i]
            keep_i, gain_i = keep_ref[i], gain_ref[i]
            e_ref[0, i] = keep_i * e_ref[0, i] + gain_i * ((hz - hz_j) - (hy - hy_k))
            e_ref[1, i] = keep_i * e_ref[1, i] + gain_i * ((hx - hx_k) - (hz - hz_i))
            e_ref[2, i] = keep_i * e_ref[2, i] + gain_i * (((hy - hy_i) - (hx - hx_j)) - current)

        for i in range(7):
            update_h(i, e_ref[1, i + 1], e_ref[2, i + 1], (0, 1))
        update_h(7, None, None, (0,))
        if n == 0:
            for copy in coef_copies:
                copy.wait_recv()
            for g in range(nz):
                gather_buf[g * cap : (g + 1) * cap, :] = coef_recv[g]
            fields(gather_buf[...], [0, ITERS])
        e_0 = [e_ref[c, 0] for c in range(3)]
        def inner(n=n, hx_y=hx_y, hz_y=hz_y, h_z=h_z):
            for i in range(1, 7):
                update_e(i, h_ref[1, i - 1], h_ref[2, i - 1], hx_y, hz_y, h_z)

        if n > 0:
            inner()

        wait_recv([m for m in FAR if m not in LATE], n)
        ex_m, ey_m, ez_m = got(4), got(5), got(6)
        ey_p, ez_p = got(8), got(9)
        ex_edge = got(11)
        if n > 0:
            ex_m, ez_p, ex_edge = ex_m + was_owed[0], ez_p + was_owed[1], ex_edge + was_owed[2]
        ex_k = jnp.where(lane == 127, 0.0, pltpu.roll(ex_m, 127, 1))
        ex_j = jnp.where(row == 7, ex_edge, pltpu.roll(ex_m, 7, 0))
        hy_x = -0.5 * ((ex_k - ex_m) - (e_0[2] - ez_m)) * low[0]
        hz_x = -0.5 * ((e_0[1] - ey_m) - (ex_j - ex_m)) * low[0]
        if n > 0:
            hy_x, hz_x = hy_x + ghosts[0], hz_x + ghosts[1]
        update_e(0, hy_x, hz_x, hx_y, hz_y, h_z)
        if n < ITERS - 1:
            pack_low(n + 1)
            send(LOW, n + 1)
        update_h(7, ey_p, ez_p, (1,))
        hz_y = hz_y - jnp.where(row == 7, 0.5 * low[1] * got(13), 0.0)
        ghosts = [hy_x, hz_x, hx_y, hz_y, h_z]
        update_e(7, h_ref[1, 6], h_ref[2, 6], hx_y, hz_y, h_z)

        if n < ITERS - 1:
            pack_high(n + 1)
            send(HIGH, n + 1)
            pack_edges(n + 1)
            send(EDGES, n + 1)
            owed[:3] = [
                lacking(lane == 0, 7, pltpu.roll(g_m, 112, 1)),
                lacking(lane == 127, 10, pltpu.roll(zp, 120, 1)),
                lacking(jnp.logical_and(lane == 0, row == 7), 12, pltpu.roll(g_edge, 112, 1)),
            ]
        if n == 0:
            inner()
        if n == 0 and ITERS > 1:
            fields(gather_buf[...], [k for k in range(2 * ITERS) if k not in (0, ITERS)])

        wait_recv(LATE, n)
        x_edge, z_edge = got(0), got(2)
        if n > 0:
            x_edge = x_edge + lacking(lane == 127, 1, was_owed[3])
            z_edge = z_edge + lacking(lane == 23, 3, was_owed[4])
        x_edge = jnp.where(lane == 127, 0.5 * low[0] * x_edge, 0.0)
        z_edge = jnp.where(lane == 23, 0.5 * low[2] * z_edge, 0.0)
        ghosts[0] = ghosts[0] - x_edge
        ghosts[4] = ghosts[4] + pltpu.roll(z_edge, 112, 1)
        e_ref[2, 0] = e_ref[2, 0] + gain_ref[0] * x_edge
        e_ref[0, 7] = e_ref[0, 7] + gain_ref[7] * pltpu.roll(z_edge, 105, 1)

        if n < ITERS - 1:
            if n == ITERS - 2:
                voltages(n + 1)
                volt_copies = send_voltages()
            pack_near(n + 1)
            send(NEAR, n + 1)
            if n < ITERS - 2:
                voltages(n + 1)

    final = base_ref[...]
    pick = first[:slots]
    rows = [
        jnp.where(
            pick,
            jnp.broadcast_to(drive[0:1], final.shape),
            jnp.broadcast_to(drive[1:2], final.shape),
        )
        for drive in reversed(drives)
    ]
    for copy in volt_copies:
        copy.wait_recv()
    for g in range(nz):
        gather_buf[g * cap : (g + 1) * cap, :] = volt_recv[g]
    table = gather_buf[...]
    for k in range(ITERS):
        final = final + rows[k] * table[:, k : k + 1]
    base_ref[...] = final
    for copy in coef_copies + volt_copies:
        copy.wait_send()
    for n in range(ITERS):
        wait_send(n)


def hand_out(*refs):
    sources, results, sem = refs[:3], refs[3:6], refs[6]
    copies = [
        pltpu.make_async_copy(src, dst, sem.at[n])
        for n, (src, dst) in enumerate(zip(sources, results))
    ]
    for copy in copies:
        copy.start()
    for copy in copies:
        copy.wait()


def solution(mesh):
    sizes = tuple(mesh.shape[a] for a in AXES)

    def local(
        e_field,
        material,
        permittivity,
        loss,
        port_cell,
        port_owner,
        circuit_block,
        circuit_state,
        mna_update,
        mna_drive,
        mna_sense,
    ):
        slots, nodes = circuit_state.shape
        cap = slots // sizes[2]
        hbm = pl.BlockSpec(memory_space=pltpu.HBM)
        dma = pltpu.SemaphoreType.DMA
        vmem = pl.BlockSpec(memory_space=pltpu.VMEM)
        shapes = (e_field.shape, e_field.shape, circuit_state.shape)
        results = pl.pallas_call(
            functools.partial(kernel, sizes),
            out_shape=[pltpu.VMEM(shape, F32) for shape in shapes],
            in_specs=[hbm] * 11,
            out_specs=[vmem] * 3,
            scratch_shapes=[
                pltpu.SMEM(permittivity.shape, F32),
                pltpu.SMEM(loss.shape, F32),
                pltpu.SMEM(port_cell.shape, jnp.int32),
                pltpu.SMEM(port_cell.shape, jnp.int32),
                pltpu.SMEM(circuit_block.shape, jnp.int32),
                pltpu.VMEM(material.shape, jnp.int32),
                pltpu.VMEM(material.shape, F32),
                pltpu.VMEM(material.shape, F32),
                pltpu.VMEM((ITERS,) + material.shape, F32),
                pltpu.VMEM((64, 2 * ITERS * 128), F32),
                pltpu.VMEM(circuit_state.shape, F32),
                pltpu.VMEM(mna_update.shape, F32),
                pltpu.VMEM(mna_drive.shape, F32),
                pltpu.VMEM(mna_sense.shape, F32),
                pltpu.VMEM((ITERS, TILES, 8, 128), F32),
                pltpu.VMEM((ITERS, TILES, 8, 128), F32),
                pltpu.VMEM((sizes[2], cap, 128), F32),
                pltpu.VMEM((sizes[2], cap, 128), F32),
                pltpu.VMEM((sizes[2], cap, 128), F32),
                pltpu.VMEM((sizes[2], cap, 128), F32),
                pltpu.VMEM((slots, 128), F32),
                dma((11,)),
                dma((ITERS, len(MESSAGES))),
                dma((ITERS, len(MESSAGES))),
                dma((sizes[2],)),
                dma((sizes[2],)),
                dma((sizes[2],)),
                dma((sizes[2],)),
                pltpu.SemaphoreType.REGULAR,
                pltpu.SemaphoreType.REGULAR,
            ],
            compiler_params=pltpu.CompilerParams(
                collective_id=0, has_side_effects=True, vmem_limit_bytes=32 * 1024 * 1024
            ),
        )(
            *(
                pltpu.with_memory_space_constraint(array, pltpu.HBM)
                for array in (
                    e_field,
                    material,
                    permittivity,
                    loss,
                    port_cell,
                    port_owner.reshape(-1),
                    circuit_block,
                    circuit_state,
                    mna_update,
                    mna_drive,
                    mna_sense,
                )
            )
        )
        return pl.pallas_call(
            hand_out,
            out_shape=[jax.ShapeDtypeStruct(shape, F32) for shape in shapes],
            in_specs=[vmem] * 3,
            out_specs=[hbm] * 3,
            scratch_shapes=[dma((3,))],
        )(*(pltpu.with_memory_space_constraint(r, pltpu.VMEM) for r in results))

    placed = (
        P(None, "gx", "gy", "gz"),
        P("gx", "gy", "gz"),
        P(),
        P(),
        P(("gx", "gy", "gz")),
        P(("gx", "gy", "gz"), None),
        P(("gx", "gy", "gz")),
        P(("gx", "gy", "gz"), None),
        P(("gx", "gy", "gz"), None, None),
        P(("gx", "gy", "gz"), None),
        P(("gx", "gy", "gz"), None),
    )
    return jax.shard_map(
        local,
        mesh=mesh,
        in_specs=placed,
        out_specs=(
            P(None, "gx", "gy", "gz"),
            P(None, "gx", "gy", "gz"),
            P(("gx", "gy", "gz"), None),
        ),
        check_vma=False,
    )
```
